1024 devices in a mesh: dp: 16 (over y, core), expert: 64 (over x, z).
Axes of the slice: x: 8, y: 8, z: 8, core: 2. Of those that a mesh axis runs over, the one named last changes fastest.
Arguments:
- layer_input: bfloat16 [32768, 4096], P(('dp', 'expert')), may hold values from -6 to 6
- out_grad: bfloat16 [32768, 4096], P(('dp', 'expert')), may hold values from -6 to 6
- expert_ids: int32 [131072, 2], P(('dp', 'expert')), may hold values from 0 to 63, all different within a row; in each aligned block of 128 rows (0 to 127, 128 to 255, ...) at most 5 rows name the same one
- gates: bfloat16 [131072, 2], P(('dp', 'expert')), may hold values from 0.099609375 to 0.8984375
- up_weight: bfloat16 [64, 1024, 1024], P('expert'), may hold values from -0.1875 to 0.1875
- down_weight: bfloat16 [64, 1024, 1024], P('expert'), may hold values from -0.1875 to 0.1875
Outputs:
- input_grad: bfloat16 [32768, 4096], P(('dp', 'expert'))
- gate_grad: bfloat16 [131072, 2], P(('dp', 'expert'))
- up_grad: float32 [64, 1024, 1024], P('expert', 'dp')
- down_grad: float32 [64, 1024, 1024], P('expert', 'dp')
The draws below stay inside these ranges and needn't reach their ends.
Inputs may be any that keep to these rules, and one draw needn't show every extreme that they name: `expert_ids`: within the 128 sub-tokens of one device, each expert is chosen by at most 5 of them, and some expert reaches 5 in some device's rows; the 2 experts of a sub-token differ.
All inputs are finite; a program needn't handle non-finite values.
Results may differ from the reference program's by a relative error of at most 0.023.
Values may be sent and summed in bfloat16 or wider, within the bound.
No kernel may reach another device: no remote copies, remote signals or barrier semaphores. Data moves between devices by JAX's collectives and lax.ppermute only.
A program may use at most 32 MiB of HBM per device.

```python
import math
import jax
import jax.numpy as jnp
import numpy as np
from jax import lax

D = 4096
SUB = 4
DS = 1024
HID = 1024
TOP = 2
TOK_DEV = 32
EXPERTS = 64
CAP = 5
TOKENS = 32768
SUBTOK = 131072
N_DP = 16
N_EXPERT = 64


def block_scale(own_key, shape, cuts, smallest, largest):
    gain, own = 1.0, jax.random.fold_in(own_key, 6)
    for dim, parts in cuts:
        steps = jnp.exp(jax.random.uniform(jax.random.fold_in(own, dim), (parts,), jnp.float32, smallest / len(cuts), largest / len(cuts)))
        gain = gain * jnp.repeat(steps, shape[dim] // parts).reshape([-1 if axis == dim else 1 for axis in range(len(shape))])
    return gain


def deal_out(key, own, number, rows, number_of, top, bound, slope):
    order = jax.random.permutation(key, number_of)
    packed, usual = shares(number_of, rows * top, bound, slope, True), shares(number_of, rows * top, bound, slope, False)
    places = jnp.arange(number_of)

    def named(tallies, rotation):
        used = int((tallies > 0).sum())
        fixed = max(1, used // 4)
        passed = fixed + (places - fixed + rotation * (used - fixed)) % max(1, number_of - fixed)
        return jnp.zeros((number_of,), jnp.int32).at[order[jnp.where(places < fixed, places, passed)]].set(jnp.asarray(tallies, jnp.int32))

    tallies = jnp.where(number % 4 == 0, named(packed, number // 4), named(usual, number - number // 4 - 1))
    mixed = jax.random.permutation(jax.random.fold_in(own, 3), number_of)
    giver, receiver = mixed[0:number_of // 2 * 2:2], mixed[1:number_of // 2 * 2:2]
    slack = jnp.minimum(tallies[giver] - 1, bound - tallies[receiver]) // 2
    slack = jnp.where((giver == order[0]) | (receiver == order[0]) | (tallies[receiver] == 0), 0, jnp.maximum(slack, 0))
    passed = jax.random.randint(jax.random.fold_in(own, 4), (number_of // 2,), 0, 1 << 20) % (slack + 1)
    tallies = tallies.at[giver].add(-passed).at[receiver].add(passed)
    labels = jnp.searchsorted(jnp.cumsum(tallies), jnp.arange(rows * top), side="right").astype(jnp.int32)
    table = labels.reshape(top, rows).T
    table = table[jax.random.permutation(jax.random.fold_in(own, 1), rows)]
    rotation = jax.random.randint(jax.random.fold_in(own, 2), (rows, 1), 0, top)
    return jnp.take_along_axis(table, (jnp.arange(top)[None, :] + rotation) % top, axis=1)


def shares(amount, total, limit, lean, full):
    weights = [(1 << 20) // math.isqrt(grade ** lean) + 1 for grade in range(1, amount + 1)]
    largest = limit if full else min(limit, max(-(-total // amount), total * weights[0] // sum(weights)))
    least = 1 if total - largest >= amount - 1 else 0
    counts, surplus = [largest] + [least] * (amount - 1), total - largest - least * (amount - 1)
    while surplus > 0:
        free = [i for i in range(1, amount) if counts[i] < largest] or [i for i in range(1, amount) if counts[i] < limit]
        mass, remaining = sum([weights[i] for i in free]), surplus
        for i in free:
            extra = min(limit - counts[i], max(1, remaining * weights[i] // mass), surplus)
            counts[i] = counts[i] + extra
            surplus = surplus - extra
    return np.array(counts)


def noise(key, shape, width, bound, shards=(), held_as=jnp.bfloat16):
    factor_of = block_scale(key, shape, shards, -0.22, 0.18) if shards else 1.0
    entries = jax.random.normal(key, shape, jnp.float32) * width * factor_of
    return jnp.minimum(jnp.maximum(entries, -bound), bound).astype(held_as)


def setup_inputs(seed: int = 0) -> dict:
    key_of = jax.random.split(jax.random.key(seed), 7)
    layer_input = noise(key_of[0], (TOKENS, D), 1.0, 6.0, ((0, 1024),))
    out_grad = noise(key_of[1], (TOKENS, D), 1.0, 6.0, ((0, 1024),))
    expert_ids_keys = jax.random.split(jax.random.fold_in(key_of[2], 1), SUBTOK // (TOK_DEV * SUB))
    expert_ids_turns = jax.random.permutation(jax.random.fold_in(key_of[2], 3), SUBTOK // (TOK_DEV * SUB))
    expert_ids = jax.vmap(lambda own, number: deal_out(jax.random.fold_in(key_of[2], 2), own, number, TOK_DEV * SUB, EXPERTS, TOP, CAP, 2))(expert_ids_keys, expert_ids_turns).reshape((SUBTOK, TOP))
    gates = jnp.clip(0.099609375 + 0.7988281 * jax.random.uniform(key_of[3], (SUBTOK, TOP), jnp.float32) ** block_scale(key_of[3], (SUBTOK, TOP), ((0, 1024),), -0.2, 0.2), 0.099609375, 0.8984375).astype(jnp.bfloat16)
    up_weight = noise(key_of[4], (EXPERTS, DS, HID), DS ** -0.5, 0.1875, ((0, 64),))
    down_weight = noise(key_of[5], (EXPERTS, HID, DS), HID ** -0.5, 0.1875, ((0, 64),))
    return dict(layer_input=layer_input, out_grad=out_grad, expert_ids=expert_ids, gates=gates, up_weight=up_weight, down_weight=down_weight)


def silu_slope(pre_act):
    sig_val = jax.nn.sigmoid(pre_act)
    return sig_val * (1.0 + pre_act * (1.0 - sig_val))


def reference(layer_input, out_grad, expert_ids, gates, up_weight, down_weight):
    devices = N_DP * N_EXPERT
    sub_in = layer_input.reshape(-1, DS)
    sub_grad = out_grad.reshape(-1, DS)
    n_rows = sub_in.shape[0]
    block = n_rows // devices
    flat_ids = expert_ids.reshape(devices, block * TOP).astype(jnp.int32)
    onehot = (flat_ids[:, :, None] == jnp.arange(EXPERTS, dtype=jnp.int32)[None, None, :]).astype(jnp.int32)
    before = jnp.cumsum(onehot, axis=1) - onehot
    slots = jnp.sum(before * onehot, axis=2)
    owners = jnp.arange(devices, dtype=jnp.int32)[:, None]
    position = ((flat_ids * devices + owners) * CAP + slots).reshape(-1)
    n_assign = n_rows * TOP
    table = jnp.full((EXPERTS * devices * CAP,), n_assign, jnp.int32)
    table = table.at[position].set(jnp.arange(n_assign, dtype=jnp.int32))
    table = table.reshape(EXPERTS, devices * CAP)
    flat_gates = gates.reshape(-1)

    def expert_step(carry, item):
        input_acc, gate_acc = carry
        index, w_up, w_down = item
        live = index < n_assign
        safe = jnp.where(live, index, 0)
        rows = safe // TOP
        features = jnp.where(live[:, None], sub_in[rows], jnp.zeros((), jnp.bfloat16))
        upstream = jnp.where(live[:, None], sub_grad[rows], jnp.zeros((), jnp.bfloat16))
        gate_vals = jnp.where(live, flat_gates[safe], jnp.zeros((), jnp.bfloat16)).astype(jnp.float32)[:, None]
        pre_act = jnp.dot(features, w_up, preferred_element_type=jnp.float32)
        hidden = jax.nn.silu(pre_act).astype(jnp.bfloat16)
        back_proj = jnp.dot(upstream, w_down.T, preferred_element_type=jnp.float32)
        gate_part = jnp.sum(hidden.astype(jnp.float32) * back_proj, axis=1)
        scaled = (gate_vals * upstream.astype(jnp.float32)).astype(jnp.bfloat16)
        hidden_grad = (gate_vals * back_proj * silu_slope(pre_act)).astype(jnp.bfloat16)
        pieces = jnp.dot(hidden_grad, w_up.T, preferred_element_type=jnp.float32).astype(jnp.bfloat16)
        target = jnp.where(live, rows, n_rows)
        input_acc = input_acc.at[target].add(pieces.astype(jnp.float32), mode="drop")
        gate_acc = gate_acc.at[jnp.where(live, index, n_assign)].set(gate_part, mode="drop")
        feat_grp = features.reshape(N_DP, -1, DS).astype(jnp.float32)
        hgrad_grp = hidden_grad.reshape(N_DP, -1, HID).astype(jnp.float32)
        hid_grp = hidden.reshape(N_DP, -1, HID).astype(jnp.float32)
        scaled_grp = scaled.reshape(N_DP, -1, DS).astype(jnp.float32)
        up_part = jnp.einsum("gra,grb->gab", feat_grp, hgrad_grp).astype(jnp.bfloat16)
        down_part = jnp.einsum("gra,grb->gab", hid_grp, scaled_grp).astype(jnp.bfloat16)
        up_sum = jnp.sum(up_part.astype(jnp.float32), axis=0)
        down_sum = jnp.sum(down_part.astype(jnp.float32), axis=0)
        return (input_acc, gate_acc), (up_sum, down_sum)

    start = (jnp.zeros((n_rows, DS), jnp.float32), jnp.zeros((n_assign,), jnp.float32))
    (input_acc, gate_acc), (up_grad, down_grad) = lax.scan(expert_step, start, (table, up_weight, down_weight))
    input_grad = input_acc.astype(jnp.bfloat16).reshape(-1, D)
    gate_grad = gate_acc.astype(jnp.bfloat16).reshape(n_rows, TOP)
    return (input_grad, gate_grad, up_grad, down_grad)
```

```python
import functools

import jax
import jax.numpy as jnp
from jax import lax
from jax.experimental import pallas as pl
from jax.experimental.pallas import tpu as pltpu
from jax.sharding import PartitionSpec as P

TOP = 2
SUB = 4
CAP = 5
LANE = 128
ROWS8 = 8
F32 = jnp.float32
BF16 = jnp.bfloat16
VMEM = pl.BlockSpec(memory_space=pltpu.VMEM)
SMEM = pl.BlockSpec(memory_space=pltpu.SMEM)


def iota(shape, dim):
    return lax.broadcasted_iota(jnp.int32, shape, dim)


def one_hot(mask):
    return jnp.where(mask, 1.0, 0.0).astype(BF16)


def mm(left, right):
    return jnp.dot(left, right, preferred_element_type=F32)


def mm_tr(left, right):
    return lax.dot_general(left, right, (((1,), (1,)), ((), ())), preferred_element_type=F32)


def tr_mm(left, right):
    return lax.dot_general(left, right, (((0,), (0,)), ((), ())), preferred_element_type=F32)


def by_sublane(peers):
    size = peers * ROWS8
    row, col = iota((size, size), 0), iota((size, size), 1)
    return one_hot(col == lax.rem(row, peers) * ROWS8 + lax.div(row, peers))


def by_peer(peers):
    size = peers * ROWS8
    row, col = iota((size, size), 0), iota((size, size), 1)
    return one_hot(col == lax.rem(row, ROWS8) * peers + lax.div(row, ROWS8))


def natural_order(block):
    tokens = block // SUB
    row, col = iota((block, block), 0), iota((block, block), 1)
    return one_hot(row == lax.rem(col, tokens) * SUB + lax.div(col, tokens))


def dispatch_kernel(x_ref, g_ref, ids_ref, gates_ref, out_ref, s_ref, rows, picks, packed):
    tokens = x_ref.shape[0]
    block = ids_ref.shape[1]
    peers = out_ref.shape[0] // ROWS8
    width = rows.shape[1]
    chunks = width // LANE
    top = jnp.concatenate(
        [ids_ref[...].astype(F32), gates_ref[...].astype(F32), jnp.zeros((4, block), F32)], axis=0
    ).astype(BF16)
    top = mm(top, natural_order(block))
    expert = iota((peers, block), 0).astype(F32)
    hot = [expert == top[k : k + 1] for k in range(TOP)]
    chosen = one_hot(hot[0] | hot[1])
    earlier = one_hot(iota((block, block), 0) < iota((block, block), 1))
    before = mm(chosen, earlier)
    weight = jnp.where(hot[0], top[2:3], jnp.where(hot[1], top[3:4], 0.0))
    for c in range(CAP):
        slot = pl.ds(c * peers, peers)
        here = before == float(c)
        for k in range(TOP):
            s_ref[k, slot, :] = one_hot(hot[k] & here)
        picks[0, slot, :] = one_hot((hot[0] | hot[1]) & here)
        picks[1, slot, :] = jnp.where(here, weight, 0.0).astype(BF16)
    for a, ref in enumerate((x_ref, g_ref)):
        for j in range(SUB):
            rows[j * tokens : (j + 1) * tokens, :] = ref[:, j * width : (j + 1) * width]
        sent = mm(picks[a], rows[...]).astype(BF16)
        for c in range(CAP):
            for j in range(chunks):
                packed[j * peers : (j + 1) * peers, (a * CAP + c) * LANE : (a * CAP + c + 1) * LANE] = (
                    sent[c * peers : (c + 1) * peers, j * LANE : (j + 1) * LANE]
                )
    out_ref[...] = mm(by_peer(peers), packed[...]).astype(BF16)


def unpack(source, target, peers, base):
    chunks = target.shape[1] // LANE
    for c in range(CAP):
        for j in range(chunks):
            target[c * peers : (c + 1) * peers, j * LANE : (j + 1) * LANE] = source[
                j * peers : (j + 1) * peers, (base + c) * LANE : (base + c + 1) * LANE
            ]


def expert_kernel(
    order, place_ref, in_ref, up_ref, down_ref, hg_ref, gate_ref, *rest
):
    n_chip = len(order)
    mine, theirs = rest[:n_chip], rest[n_chip : n_chip + 2]
    feat, scal, hid, left = rest[n_chip + 2 :]
    peers = in_ref.shape[0] // ROWS8
    width = up_ref.shape[0]
    chip, core = place_ref[0], place_ref[1]
    moved = mm(by_sublane(peers), in_ref[...]).astype(BF16)
    unpack(moved, feat, peers, 0)
    unpack(moved, scal, peers, CAP)
    pre = mm(feat[...], up_ref[...])
    sig = jax.nn.sigmoid(pre)
    hidden = (pre * sig).astype(BF16)
    hid[...] = hidden
    back = mm_tr(scal[...], down_ref[...])
    part = jnp.sum(hidden.astype(F32) * back, axis=1, keepdims=True)
    gate_ref[...] = jnp.broadcast_to(part, gate_ref.shape).astype(BF16)
    hg_ref[...] = (back * (sig * (1.0 + pre * (1.0 - sig)))).astype(BF16)
    piece = width // n_chip
    half = piece // 2
    first = core == 0
    for a, (source, right) in enumerate(((feat, hg_ref), (hid, scal))):
        for i, p in enumerate(order):
            at = lax.rem(chip + p, n_chip) * piece
            left[:, i * piece : (i + 1) * piece] = source[:, pl.ds(pl.multiple_of(at, piece), piece)]
        lanes = slice(a * width, (a + 1) * width)
        for i in range(0, n_chip, 2):
            total = tr_mm(left[:, i * piece : (i + 2) * piece], right[...]).astype(BF16)
            for h in range(2):
                low = total[h * piece : h * piece + half]
                high = total[h * piece + half : (h + 1) * piece]
                mine[order[i + h]][:, lanes] = jnp.where(first, low, high)
                other = jnp.where(first, high, low)
                if i == 0:
                    theirs[0][h * half : (h + 1) * half, lanes] = other
                else:
                    row = (i - 2 + h) * half
                    theirs[1][row : row + half, lanes] = other


def piece_kernel(hg_ref, up_ref, gate_ref, out_ref, packed):
    peers = out_ref.shape[0] // ROWS8
    width = up_ref.shape[0]
    chunks = width // LANE
    piece = mm_tr(hg_ref[...], up_ref[...]).astype(BF16)
    for c in range(CAP):
        for j in range(chunks):
            packed[j * peers : (j + 1) * peers, c * LANE : (c + 1) * LANE] = piece[
                c * peers : (c + 1) * peers, j * LANE : (j + 1) * LANE
            ]
    packed[: CAP * peers, CAP * LANE :] = gate_ref[...]
    packed[CAP * peers :, CAP * LANE :] = jnp.zeros((packed.shape[0] - CAP * peers, LANE), BF16)
    out_ref[...] = mm(by_peer(peers), packed[...]).astype(BF16)


def combine_kernel(in_ref, s_ref, gates_ref, grad_ref, gate_ref, pieces):
    peers = in_ref.shape[0] // ROWS8
    tokens = grad_ref.shape[0]
    width = pieces.shape[1]
    block = s_ref.shape[2]
    moved = mm(by_sublane(peers), in_ref[...]).astype(BF16)
    unpack(moved, pieces, peers, 0)
    picks = s_ref[0] + s_ref[1]
    total = tr_mm(picks, pieces[...]).astype(BF16)
    for j in range(SUB):
        grad_ref[:, j * width : (j + 1) * width] = total[j * tokens : (j + 1) * tokens, :]
    gates = moved[: CAP * peers, CAP * LANE :]
    rows = [tr_mm(gates, s_ref[k])[0:1] for k in range(TOP)]
    rows = jnp.concatenate(rows + [jnp.zeros((8 - TOP, block), F32)], axis=0).astype(BF16)
    rows = mm_tr(rows, natural_order(block))
    gate_ref[...] = (rows[:TOP] / gates_ref[...].astype(F32)).astype(BF16)


def call(kernel, out, ins, scratch, flops=0, moved=0):
    return pl.pallas_call(
        kernel,
        out_shape=out,
        in_specs=ins,
        out_specs=jax.tree.map(lambda _: VMEM, out),
        scratch_shapes=scratch,
        compiler_params=pltpu.CompilerParams(vmem_limit_bytes=40 << 20),
        cost_estimate=pl.CostEstimate(flops=flops, bytes_accessed=moved, transcendentals=0),
    )


def shape(*dims, dtype=BF16):
    return jax.ShapeDtypeStruct(dims, dtype)


def dispatch(layer_input, out_grad, ids, gates, peers, width):
    tokens = layer_input.shape[0]
    block = tokens * SUB
    rows = peers * CAP
    return call(
        dispatch_kernel,
        (shape(peers * ROWS8, 2 * CAP * LANE), shape(TOP, rows, block)),
        [VMEM] * 4,
        [
            pltpu.VMEM((block, width), BF16),
            pltpu.VMEM((2, rows, block), BF16),
            pltpu.VMEM((peers * ROWS8, 2 * CAP * LANE), BF16),
        ],
        flops=10**9,
        moved=4 << 20,
    )(layer_input, out_grad, ids, gates)


def expert(place, received, w_up, w_down, order):
    peers = received.shape[0] // ROWS8
    width = w_up.shape[0]
    rows = peers * CAP
    n_chip = len(order)
    half = width // n_chip // 2
    outs = (
        (shape(rows, width), shape(rows, LANE))
        + tuple(shape(half, 2 * width) for _ in order)
        + (shape(2 * half, 2 * width), shape((n_chip - 2) * half, 2 * width))
    )
    out = call(
        functools.partial(expert_kernel, order),
        outs,
        [SMEM, VMEM, VMEM, VMEM],
        [pltpu.VMEM((rows, width), BF16)] * 4,
        flops=4 * 10**9,
        moved=10 << 20,
    )(place, received, w_up, w_down)
    return out[0], out[1], out[2 : 2 + n_chip], out[2 + n_chip], out[3 + n_chip]


def give_back(hidden_grad, w_up, gate_part):
    rows, width = hidden_grad.shape
    peers = rows // CAP
    size = (peers * ROWS8, (CAP + 1) * LANE)
    return call(
        piece_kernel,
        shape(*size),
        [VMEM] * 3,
        [pltpu.VMEM(size, BF16)],
        flops=10**9,
        moved=4 << 20,
    )(hidden_grad, w_up, gate_part)


def combine(returned, picks, gates, tokens, width):
    return call(
        combine_kernel,
        (shape(tokens, SUB * width), shape(TOP, tokens * SUB)),
        [VMEM] * 3,
        [pltpu.VMEM((picks.shape[1], width), BF16)],
        flops=10**9,
        moved=2 << 20,
    )(returned, picks, gates)


def added(*terms):
    total = terms[0].astype(F32)
    for term in terms[1:]:
        total = total + term.astype(F32)
    return total


def body(n_dp, layer_input, out_grad, expert_ids, gates, up_weight, down_weight):
    tokens = layer_input.shape[0]
    width = up_weight.shape[1]
    peers = lax.axis_size("expert")
    n_chip = n_dp // 2
    at = lax.axis_index("dp")
    place = jnp.stack([at // 2, at % 2]).astype(jnp.int32)
    gates_t = gates.T
    w_up, w_down = up_weight[0], down_weight[0]

    def exchange(array):
        moved = lax.all_to_all(
            array.reshape(peers, ROWS8, -1), "expert", split_axis=0, concat_axis=0, tiled=True
        )
        return moved.reshape(array.shape)

    def hop(array, step):
        return lax.ppermute(array, "dp", [(i, (i + 2 * step) % n_dp) for i in range(n_dp)])

    def swap(array):
        return lax.ppermute(array, "dp", [(i, i ^ 1) for i in range(n_dp)])

    sent, picks = dispatch(layer_input, out_grad, expert_ids.T, gates_t, peers, width)
    received = exchange(sent)
    half_way = n_chip // 2
    order = [half_way]
    for step in range(half_way - 1, 0, -1):
        order += [n_chip - step, step]
    order.append(0)
    hidden_grad, gate_part, mine, theirs_first, theirs = expert(
        place, received, w_up, w_down, order
    )
    returned = exchange(give_back(hidden_grad, w_up, gate_part))
    got_first, got = swap(theirs_first), swap(theirs)
    half = theirs_first.shape[0] // 2

    def own(offset):
        i = order.index(offset)
        if i < 2:
            return [mine[i_of[offset]], got_first[i * half : (i + 1) * half]]
        return [mine[i_of[offset]], got[(i - 2) * half : (i - 1) * half]]

    i_of = {p: p for p in order}
    up, down = None, None
    for step in range(half_way, 0, -1):
        terms = own(step) + ([] if up is None else [up])
        up = hop(added(*terms).astype(BF16), 1)
        if step > 1:
            terms = own(n_chip - step + 1) + ([] if down is None else [down])
            down = hop(added(*terms).astype(BF16), -1)
    total = added(*own(0), up, down)
    input_grad, gate_grad = combine(returned, picks, gates_t, tokens, width)
    return (input_grad, gate_grad.T, total[None, :, :width], total[None, :, width:])


def solution(mesh):
    placed = (
        P(("dp", "expert"), None),
        P(("dp", "expert"), None),
        P(("dp", "expert"), None),
        P(("dp", "expert"), None),
        P("expert", None, None),
        P("expert", None, None),
    )
    return jax.shard_map(
        functools.partial(body, mesh.shape["dp"]),
        mesh=mesh,
        in_specs=placed,
        out_specs=(
            P(("dp", "expert"), None),
            P(("dp", "expert"), None),
            P("expert", "dp", None),
            P("expert", "dp", None),
        ),
        check_vma=False,
    )
```

```python
import functools

import jax
import jax.numpy as jnp
from jax import lax
from jax.experimental import pallas as pl
from jax.experimental.pallas import tpu as pltpu
from jax.sharding import PartitionSpec as P

TOP = 2
SUB = 4
CAP = 5
LANE = 128
ROWS8 = 8
N_CHIP = 8
F32 = jnp.float32
BF16 = jnp.bfloat16
VMEM = pl.BlockSpec(memory_space=pltpu.VMEM)
SMEM = pl.BlockSpec(memory_space=pltpu.SMEM)
HBM = pl.BlockSpec(memory_space=pltpu.HBM)
ANY = pl.BlockSpec(memory_space=pl.ANY)


def iota(shape, dim):
    return lax.broadcasted_iota(jnp.int32, shape, dim)


def one_hot(mask):
    return jnp.where(mask, 1.0, 0.0).astype(BF16)


def mm(left, right):
    return jnp.dot(left, right, preferred_element_type=F32)


def mm_tr(left, right):
    return lax.dot_general(left, right, (((1,), (1,)), ((), ())), preferred_element_type=F32)


def tr_mm(left, right):
    return lax.dot_general(left, right, (((0,), (0,)), ((), ())), preferred_element_type=F32)


def by_sublane(peers):
    size = peers * ROWS8
    row, col = iota((size, size), 0), iota((size, size), 1)
    return one_hot(col == lax.rem(row, peers) * ROWS8 + lax.div(row, peers))


def by_peer(peers):
    size = peers * ROWS8
    row, col = iota((size, size), 0), iota((size, size), 1)
    return one_hot(col == lax.rem(row, ROWS8) * peers + lax.div(row, ROWS8))


def natural_order(block):
    tokens = block // SUB
    row, col = iota((block, block), 0), iota((block, block), 1)
    return one_hot(row == lax.rem(col, tokens) * SUB + lax.div(col, tokens))


def dispatch_kernel(
    x_hbm, g_hbm, ids_hbm, gates_hbm, out_ref, s_ref,
    x_ref, g_ref, ids_ref, gates_ref, rows, picks, packed, sems,
):
    tokens = x_ref.shape[0]
    pairs = (
        (ids_hbm, ids_ref), (gates_hbm, gates_ref), (x_hbm, x_ref), (g_hbm, g_ref),
    )
    copies = [pltpu.make_async_copy(a, b, sems.at[i]) for i, (a, b) in enumerate(pairs)]
    for copy in copies:
        copy.start()
    copies[0].wait()
    copies[1].wait()
    block = ids_ref.shape[1]
    peers = out_ref.shape[0] // ROWS8
    width = rows.shape[1]
    chunks = width // LANE
    top = jnp.concatenate(
        [ids_ref[...].astype(F32), gates_ref[...].astype(F32), jnp.zeros((4, block), F32)], axis=0
    ).astype(BF16)
    top = mm(top, natural_order(block))
    expert = iota((peers, block), 0).astype(F32)
    hot = [expert == top[k : k + 1] for k in range(TOP)]
    chosen = one_hot(hot[0] | hot[1])
    earlier = one_hot(iota((block, block), 0) < iota((block, block), 1))
    before = mm(chosen, earlier)
    weight = jnp.where(hot[0], top[2:3], jnp.where(hot[1], top[3:4], 0.0))
    for c in range(CAP):
        slot = pl.ds(c * peers, peers)
        here = before == float(c)
        for k in range(TOP):
            s_ref[k, slot, :] = one_hot(hot[k] & here)
        picks[0, slot, :] = one_hot((hot[0] | hot[1]) & here)
        picks[1, slot, :] = jnp.where(here, weight, 0.0).astype(BF16)
    for a, ref in enumerate((x_ref, g_ref)):
        copies[2 + a].wait()
        for j in range(SUB):
            rows[j * tokens : (j + 1) * tokens, :] = ref[:, j * width : (j + 1) * width]
        sent = mm(picks[a], rows[...]).astype(BF16)
        for c in range(CAP):
            for j in range(chunks):
                packed[j * peers : (j + 1) * peers, (a * CAP + c) * LANE : (a * CAP + c + 1) * LANE] = (
                    sent[c * peers : (c + 1) * peers, j * LANE : (j + 1) * LANE]
                )
    out_ref[...] = mm(by_peer(peers), packed[...]).astype(BF16)


def unpack(source, target, peers, base):
    chunks = target.shape[1] // LANE
    for c in range(CAP):
        for j in range(chunks):
            target[c * peers : (c + 1) * peers, j * LANE : (j + 1) * LANE] = source[
                j * peers : (j + 1) * peers, (base + c) * LANE : (base + c + 1) * LANE
            ]


def expert_kernel(
    order, place_ref, in_hbm, up_hbm, down_hbm, back_ref, *rest
):
    (mine_first, mine, *swapped_out), rest = rest[:4], rest[4:]
    in_ref, feat, scal, hid, hg_ref, left_up, left_down, up_ref, down_ref, packed, back_v, *rest = rest
    held, other, other_later, sems = rest
    leaving = []

    def leave(source, target):
        leaving.append(pltpu.make_async_copy(source, target, sems.at[3 + len(leaving)]))
        leaving[-1].start()

    pairs = ((in_hbm, in_ref), (up_hbm, up_ref), (down_hbm, down_ref))
    copies = [pltpu.make_async_copy(a, b, sems.at[i]) for i, (a, b) in enumerate(pairs)]
    for copy in copies:
        copy.start()
    peers = in_ref.shape[0] // ROWS8
    width = up_ref.shape[0]
    to_sublane = by_sublane(peers)
    copies[0].wait()
    moved = mm(to_sublane, in_ref[...]).astype(BF16)
    unpack(moved, feat, peers, 0)
    unpack(moved, scal, peers, CAP)
    copies[1].wait()
    pre = mm(feat[...], up_ref[...])
    sig = jax.nn.sigmoid(pre)
    hidden = (pre * sig).astype(BF16)
    hid[...] = hidden
    copies[2].wait()
    back = mm_tr(scal[...], down_ref[...])
    part = jnp.sum(hidden.astype(F32) * back, axis=1, keepdims=True)
    hg_ref[...] = (back * (sig * (1.0 + pre * (1.0 - sig)))).astype(BF16)
    piece = mm_tr(hg_ref[...], up_ref[...]).astype(BF16)
    for c in range(CAP):
        for j in range(width // LANE):
            packed[j * peers : (j + 1) * peers, c * LANE : (c + 1) * LANE] = piece[
                c * peers : (c + 1) * peers, j * LANE : (j + 1) * LANE
            ]
    rows = CAP * peers
    packed[:rows, CAP * LANE :] = jnp.broadcast_to(part, (rows, LANE)).astype(BF16)
    packed[rows:, CAP * LANE :] = jnp.zeros((packed.shape[0] - rows, LANE), BF16)
    back_v[...] = mm(by_peer(peers), packed[...]).astype(BF16)
    leave(back_v, back_ref)
    first = place_ref[1] == 0
    piece = width // N_CHIP
    half = piece // 2
    for i, p in enumerate(order):
        at = pl.ds(pl.multiple_of(lax.rem(place_ref[0] + p, N_CHIP) * piece, piece), piece)
        left_up[:, i * piece : (i + 1) * piece] = feat[:, at]
        left_down[:, i * piece : (i + 1) * piece] = hid[:, at]
    for i in range(0, N_CHIP, 2):
        for a, (left, right) in enumerate(((left_up, hg_ref), (left_down, scal))):
            total = tr_mm(left[:, i * piece : (i + 2) * piece], right[...]).astype(BF16)
            lanes = slice(a * width, (a + 1) * width)
            for h in range(2):
                low = total[h * piece : h * piece + half]
                high = total[h * piece + half : (h + 1) * piece]
                held[(i + h) * half : (i + h + 1) * half, lanes] = jnp.where(first, low, high)
                swapped, row = (other, i) if i < N_CHIP // 2 else (other_later, i - N_CHIP // 2)
                row = (row + h) * half
                swapped[row : row + half, lanes] = jnp.where(first, high, low)
        if i == 0:
            leave(held.at[pl.ds(0, half)], mine_first)
            leave(held.at[pl.ds(half, half)], mine.at[pl.ds(0, half)])
        else:
            leave(held.at[pl.ds(i * half, 2 * half)], mine.at[pl.ds((i - 1) * half, 2 * half)])
        if i == N_CHIP // 2 - 2:
            leave(other, swapped_out[0])
    leave(other_later, swapped_out[1])
    for copy in leaving:
        copy.wait()


def fetch(refs, rows, held, sems):
    copies = [
        pltpu.make_async_copy(ref.at[pl.ds(row, held.shape[1])], held.at[i], sems.at[i])
        for i, (ref, row) in enumerate(zip(refs, rows))
    ]
    for copy in copies:
        copy.start()
    for copy in copies:
        copy.wait()


def step_kernel(rows, counts, *refs):
    n_in, n_out = len(rows), len(counts)
    outs, (held, sems) = refs[-2 - n_out : -2], refs[-2:]
    fetch(refs, rows, held, sems)
    at = 0
    for out, count in zip(outs, counts):
        total = held[at].astype(F32)
        for i in range(at + 1, at + count):
            total = total + held[i].astype(F32)
        out[...] = total.astype(BF16)
        at += count


def last_kernel(width, rows, *refs):
    ins, outs, (held, sems) = refs[: len(rows)], refs[len(rows) : -2], refs[-2:]
    fetch(ins, rows, held, sems)
    for a, out in enumerate(outs):
        total = held[0, :, a * width : (a + 1) * width].astype(F32)
        for i in range(1, len(rows)):
            total = total + held[i, :, a * width : (a + 1) * width].astype(F32)
        out[...] = total


def combine_kernel(in_ref, s_ref, gates_ref, grad_ref, gate_ref, pieces):
    peers = in_ref.shape[0] // ROWS8
    tokens = grad_ref.shape[0]
    width = pieces.shape[1]
    block = s_ref.shape[2]
    moved = mm(by_sublane(peers), in_ref[...]).astype(BF16)
    unpack(moved, pieces, peers, 0)
    picks = s_ref[0] + s_ref[1]
    total = tr_mm(picks, pieces[...]).astype(BF16)
    for j in range(SUB):
        grad_ref[:, j * width : (j + 1) * width] = total[j * tokens : (j + 1) * tokens, :]
    gates = moved[: CAP * peers, CAP * LANE :]
    rows = [tr_mm(gates, s_ref[k])[0:1] for k in range(TOP)]
    rows = jnp.concatenate(rows + [jnp.zeros((8 - TOP, block), F32)], axis=0).astype(BF16)
    rows = mm_tr(rows, natural_order(block))
    gate_ref[...] = (rows[:TOP] / gates_ref[...].astype(F32)).astype(BF16)


def call(kernel, out, ins, scratch, flops, moved, limit=16, place=VMEM):
    return pl.pallas_call(
        kernel,
        out_shape=out,
        in_specs=ins,
        out_specs=jax.tree.map(lambda _: place, out),
        scratch_shapes=scratch,
        compiler_params=pltpu.CompilerParams(vmem_limit_bytes=limit << 20),
        cost_estimate=pl.CostEstimate(flops=flops, bytes_accessed=moved, transcendentals=0),
    )


def shape(*dims, dtype=BF16):
    return jax.ShapeDtypeStruct(dims, dtype)


def dispatch(layer_input, out_grad, ids, gates, peers):
    tokens, depth = layer_input.shape
    block = tokens * SUB
    rows = peers * CAP
    width = depth // SUB
    size = (peers * ROWS8, 2 * CAP * LANE)
    return call(
        dispatch_kernel,
        (shape(*size), shape(TOP, rows, block)),
        [HBM] * 4,
        [
            pltpu.VMEM((tokens, depth), BF16),
            pltpu.VMEM((tokens, depth), BF16),
            pltpu.VMEM((TOP, block), jnp.int32),
            pltpu.VMEM((TOP, block), BF16),
            pltpu.VMEM((block, width), BF16),
            pltpu.VMEM((2, rows, block), BF16),
            pltpu.VMEM(size, BF16),
            pltpu.SemaphoreType.DMA((4,)),
        ],
        flops=10**9,
        moved=4 << 20,
        limit=60,
    )(layer_input, out_grad, ids, gates)


def expert(place, received, w_up, w_down, order):
    peers = received.shape[0] // ROWS8
    width = w_up.shape[0]
    rows = peers * CAP
    half = width // N_CHIP // 2
    back = (peers * ROWS8, (CAP + 1) * LANE)
    out = call(
        functools.partial(expert_kernel, order),
        (shape(*back), shape(half, 2 * width), shape(width // 2 - half, 2 * width)) + (shape(width // 4, 2 * width),) * 2,
        [SMEM, ANY, HBM, HBM],
        [pltpu.VMEM(received.shape, BF16)]
        + [pltpu.VMEM((rows, width), BF16)] * 6
        + [
            pltpu.VMEM(w_up.shape, BF16),
            pltpu.VMEM(w_down.shape, BF16),
            pltpu.VMEM(back, BF16),
            pltpu.VMEM(back, BF16),
            pltpu.VMEM((N_CHIP * half, 2 * width), BF16),
            pltpu.VMEM((width // 4, 2 * width), BF16),
            pltpu.VMEM((width // 4, 2 * width), BF16),
            pltpu.SemaphoreType.DMA((11,)),
        ],
        flops=3 * 10**9,
        moved=8 << 20,
        limit=52,
        place=ANY,
    )(place, received, w_up, w_down)
    return out


def ring_step(half, groups, after=()):
    arrays, rows = zip(*[term for group in groups for term in group])
    width = arrays[0].shape[1]
    return call(
        functools.partial(step_kernel, rows, [len(group) for group in groups]),
        (shape(half, width),) * len(groups),
        [ANY] * (len(arrays) + len(after)),
        [pltpu.VMEM((len(arrays), half, width), BF16), pltpu.SemaphoreType.DMA((len(arrays),))],
        flops=10**6,
        moved=1 << 20,
        limit=50,
    )(*arrays, *after)


def finish(half, terms):
    arrays, rows = zip(*terms)
    width = arrays[0].shape[1]
    return call(
        functools.partial(last_kernel, width // 2, rows),
        (shape(half, width // 2, dtype=F32),) * 2,
        [ANY] * len(arrays),
        [pltpu.VMEM((len(arrays), half, width), BF16), pltpu.SemaphoreType.DMA((len(arrays),))],
        flops=10**6,
        moved=1 << 20,
        limit=50,
    )(*arrays)


def combine(returned, picks, gates, tokens, width):
    return call(
        combine_kernel,
        (shape(tokens, SUB * width), shape(TOP, tokens * SUB)),
        [VMEM] * 3,
        [pltpu.VMEM((picks.shape[1], width), BF16)],
        flops=10**10,
        moved=2 << 20,
    )(returned, picks, gates)


def body(n_dp, layer_input, out_grad, expert_ids, gates, up_weight, down_weight):
    tokens = layer_input.shape[0]
    width = up_weight.shape[1]
    peers = lax.axis_size("expert")
    at = lax.axis_index("dp")
    place = jnp.stack([at // 2, at % 2]).astype(jnp.int32)
    gates_t = gates.T
    w_up, w_down = up_weight[0], down_weight[0]

    def exchange(array):
        moved = lax.all_to_all(
            array.reshape(peers, ROWS8, -1), "expert", split_axis=0, concat_axis=0, tiled=True
        )
        return moved.reshape(array.shape)

    def hop(array, step):
        return lax.ppermute(array, "dp", [(i, (i + 2 * step) % n_dp) for i in range(n_dp)])

    def swap(array):
        return lax.ppermute(array, "dp", [(i, i ^ 1) for i in range(n_dp)])

    sent, picks = dispatch(layer_input, out_grad, expert_ids.T, gates_t, peers)
    received = exchange(sent)
    order = [N_CHIP // 2]
    for far in range(N_CHIP // 2 - 1, 0, -1):
        order += [N_CHIP - far, far]
    order.append(0)
    early = N_CHIP // 2
    back, mine_first, mine, other, other_later = expert(place, received, w_up, w_down, order)
    half = mine_first.shape[0]
    got, got_later = swap(other), swap(other_later)
    returned = exchange(back)
    input_grad, gate_grad = combine(returned, picks, gates_t, tokens, width)

    def pair(offset):
        i = order.index(offset)
        own = (mine, (i - 1) * half) if i else (mine_first, 0)
        return [own, (got, i * half) if i < early else (got_later, (i - early) * half)]

    (up,) = ring_step(half, [pair(4)])
    up = hop(up, 1)
    up, down = ring_step(half, [pair(3) + [(up, 0)], pair(5)])
    up, down = hop(up, 1), hop(down, -1)
    up, down = ring_step(half, [pair(2) + [(up, 0)], pair(6) + [(down, 0)]])
    up, down = hop(up, 1), hop(down, -1)
    up, down = ring_step(half, [pair(1) + [(up, 0)], pair(7) + [(down, 0)]], [gate_grad])
    up, down = hop(up, 1), hop(down, -1)
    up_grad, down_grad = finish(half, pair(0) + [(up, 0), (down, 0)])
    return (input_grad, gate_grad.T, up_grad[None], down_grad[None])


def solution(mesh):
    placed = (
        P(("dp", "expert"), None),
        P(("dp", "expert"), None),
        P(("dp", "expert"), None),
        P(("dp", "expert"), None),
        P("expert", None, None),
        P("expert", None, None),
    )
    return jax.shard_map(
        functools.partial(body, mesh.shape["dp"]),
        mesh=mesh,
        in_specs=placed,
        out_specs=(
            P(("dp", "expert"), None),
            P(("dp", "expert"), None),
            P("expert", "dp", None),
            P("expert", "dp", None),
        ),
        check_vma=False,
    )
```

```python
import functools

import jax
import jax.numpy as jnp
from jax import lax
from jax.experimental import pallas as pl
from jax.experimental.pallas import tpu as pltpu
from jax.sharding import PartitionSpec as P

TOP = 2
SUB = 4
CAP = 5
LANE = 128
ROWS8 = 8
N_CHIP = 8
F32 = jnp.float32
BF16 = jnp.bfloat16
VMEM = pl.BlockSpec(memory_space=pltpu.VMEM)
SMEM = pl.BlockSpec(memory_space=pltpu.SMEM)
HBM = pl.BlockSpec(memory_space=pltpu.HBM)
ANY = pl.BlockSpec(memory_space=pl.ANY)


def iota(shape, dim):
    return lax.broadcasted_iota(jnp.int32, shape, dim)


def one_hot(mask):
    return jnp.where(mask, 1.0, 0.0).astype(BF16)


def mm(left, right):
    return jnp.dot(left, right, preferred_element_type=F32)


def mm_tr(left, right):
    return lax.dot_general(left, right, (((1,), (1,)), ((), ())), preferred_element_type=F32)


def tr_mm(left, right):
    return lax.dot_general(left, right, (((0,), (0,)), ((), ())), preferred_element_type=F32)


def by_sublane(peers):
    size = peers * ROWS8
    row, col = iota((size, size), 0), iota((size, size), 1)
    return one_hot(col == lax.rem(row, peers) * ROWS8 + lax.div(row, peers))


def by_peer(peers):
    size = peers * ROWS8
    row, col = iota((size, size), 0), iota((size, size), 1)
    return one_hot(col == lax.rem(row, ROWS8) * peers + lax.div(row, ROWS8))


def natural_order(block):
    tokens = block // SUB
    row, col = iota((block, block), 0), iota((block, block), 1)
    return one_hot(row == lax.rem(col, tokens) * SUB + lax.div(col, tokens))


def dispatch_kernel(
    x_hbm, g_hbm, ids_hbm, gates_hbm, out_ref, s_ref,
    x_ref, g_ref, ids_ref, gates_ref, rows, picks, packed, sems,
):
    tokens = x_ref.shape[0]
    pairs = (
        (ids_hbm, ids_ref), (gates_hbm, gates_ref), (x_hbm, x_ref), (g_hbm, g_ref),
    )
    copies = [pltpu.make_async_copy(a, b, sems.at[i]) for i, (a, b) in enumerate(pairs)]
    for copy in copies:
        copy.start()
    copies[0].wait()
    copies[1].wait()
    block = ids_ref.shape[1]
    peers = out_ref.shape[0] // ROWS8
    width = rows.shape[1]
    chunks = width // LANE
    top = jnp.concatenate(
        [ids_ref[...].astype(F32), gates_ref[...].astype(F32), jnp.zeros((4, block), F32)], axis=0
    ).astype(BF16)
    top = mm(top, natural_order(block))
    expert = iota((peers, block), 0).astype(F32)
    hot = [expert == top[k : k + 1] for k in range(TOP)]
    chosen = one_hot(hot[0] | hot[1])
    earlier = one_hot(iota((block, block), 0) < iota((block, block), 1))
    before = mm(chosen, earlier)
    weight = jnp.where(hot[0], top[2:3], jnp.where(hot[1], top[3:4], 0.0))
    for c in range(CAP):
        slot = pl.ds(c * peers, peers)
        here = before == float(c)
        for k in range(TOP):
            s_ref[k, slot, :] = one_hot(hot[k] & here)
        picks[0, slot, :] = one_hot((hot[0] | hot[1]) & here)
        picks[1, slot, :] = jnp.where(here, weight, 0.0).astype(BF16)
    for a, ref in enumerate((x_ref, g_ref)):
        copies[2 + a].wait()
        for j in range(SUB):
            rows[j * tokens : (j + 1) * tokens, :] = ref[:, j * width : (j + 1) * width]
        sent = mm(picks[a], rows[...]).astype(BF16)
        for c in range(CAP):
            for j in range(chunks):
                packed[j * peers : (j + 1) * peers, (a * CAP + c) * LANE : (a * CAP + c + 1) * LANE] = (
                    sent[c * peers : (c + 1) * peers, j * LANE : (j + 1) * LANE]
                )
    out_ref[...] = mm(by_peer(peers), packed[...]).astype(BF16)


def unpack(source, target, peers, base):
    chunks = target.shape[1] // LANE
    for c in range(CAP):
        for j in range(chunks):
            target[c * peers : (c + 1) * peers, j * LANE : (j + 1) * LANE] = source[
                j * peers : (j + 1) * peers, (base + c) * LANE : (base + c + 1) * LANE
            ]


def hidden_kernel(place_ref, in_hbm, up_hbm, down_hbm, *refs):
    feat, scal, hid, hg_ref, part_ref, far_ref, in_ref, up_ref, down_ref, sems = refs
    pairs = ((in_hbm, in_ref), (up_hbm, up_ref), (down_hbm, down_ref))
    copies = [pltpu.make_async_copy(a, b, sems.at[i]) for i, (a, b) in enumerate(pairs)]
    for copy in copies:
        copy.start()
    peers = in_ref.shape[0] // ROWS8
    width = up_ref.shape[0]
    to_sublane = by_sublane(peers)
    copies[0].wait()
    moved = mm(to_sublane, in_ref[...]).astype(BF16)
    unpack(moved, feat, peers, 0)
    unpack(moved, scal, peers, CAP)
    copies[1].wait()
    pre = mm(feat[...], up_ref[...])
    sig = jax.nn.sigmoid(pre)
    hidden = (pre * sig).astype(BF16)
    hid[...] = hidden
    copies[2].wait()
    back = mm_tr(scal[...], down_ref[...])
    part = jnp.sum(hidden.astype(F32) * back, axis=1, keepdims=True)
    part_ref[...] = jnp.broadcast_to(part, part_ref.shape).astype(BF16)
    hg_ref[...] = (back * (sig * (1.0 + pre * (1.0 - sig)))).astype(BF16)
    here = rows_of(place_ref, N_CHIP // 2, width)
    far_ref[:, :width] = tr_mm(feat[:, here], hg_ref[...]).astype(BF16)
    far_ref[:, width:] = tr_mm(hid[:, here], scal[...]).astype(BF16)


def rows_of(place_ref, offset, width):
    piece = width // N_CHIP
    at = lax.rem(place_ref[0] + offset, N_CHIP) * piece
    return pl.ds(pl.multiple_of(at, piece), piece)


def blocks_kernel(place_ref, feat, scal, hid, hg_ref, part_ref, up_hbm, _, *refs):
    back_ref, own_ref, other_ref, up_ref, packed, back_v, left, own, other, sems = refs
    load = pltpu.make_async_copy(up_hbm, up_ref, sems.at[0])
    load.start()
    leaving = []

    def leave(source, target):
        leaving.append(pltpu.make_async_copy(source, target, sems.at[1 + len(leaving)]))
        leaving[-1].start()

    width = up_ref.shape[0]
    piece = width // N_CHIP
    half = piece // 2
    first = place_ref[1] == 0
    middle = N_CHIP // 2
    for r in range(1, middle):
        near = jnp.where(first, middle - r, middle + r)
        rows = slice((r - 1) * piece, r * piece)
        for a, (source, right) in enumerate(((feat, hg_ref), (hid, scal))):
            left[:, :piece] = source[:, rows_of(place_ref, near, width)]
            left[:, piece:] = source[:, rows_of(place_ref, N_CHIP - near, width)]
            total = tr_mm(left[...], right[...]).astype(BF16)
            lanes = slice(a * width, (a + 1) * width)
            own[rows, lanes] = total[:piece]
            other[rows, lanes] = total[piece:]
    rows = slice((middle - 1) * piece, (middle - 1) * piece + half)
    for a, (source, right) in enumerate(((feat, hg_ref), (hid, scal))):
        total = tr_mm(source[:, rows_of(place_ref, 0, width)], right[...]).astype(BF16)
        lanes = slice(a * width, (a + 1) * width)
        own[rows, lanes] = jnp.where(first, total[:half], total[half:])
        other[rows, lanes] = jnp.where(first, total[half:], total[:half])
    leave(other, other_ref)
    leave(own, own_ref)
    load.wait()
    peers = packed.shape[0] // ROWS8
    sent = mm_tr(hg_ref[...], up_ref[...]).astype(BF16)
    for c in range(CAP):
        for j in range(width // LANE):
            packed[j * peers : (j + 1) * peers, c * LANE : (c + 1) * LANE] = sent[
                c * peers : (c + 1) * peers, j * LANE : (j + 1) * LANE
            ]
    rows = CAP * peers
    packed[:rows, CAP * LANE :] = part_ref[...]
    packed[rows:, CAP * LANE :] = jnp.zeros((packed.shape[0] - rows, LANE), BF16)
    back_v[...] = mm(by_peer(peers), packed[...]).astype(BF16)
    leave(back_v, back_ref)
    for copy in leaving:
        copy.wait()


def fetch(refs, rows, held, sems):
    copies = [
        pltpu.make_async_copy(ref.at[pl.ds(row, held.shape[1])], held.at[i], sems.at[i])
        for i, (ref, row) in enumerate(zip(refs, rows))
    ]
    for copy in copies:
        copy.start()
    for copy in copies:
        copy.wait()


def step_kernel(rows, place_ref, *refs):
    ins, outs, (held, sems) = refs[: len(rows)], refs[len(rows) : -2], refs[-2:]
    fetch(ins, rows, held, sems)
    total = held[0].astype(F32)
    for i in range(1, len(rows)):
        total = total + held[i].astype(F32)
    total = total.astype(BF16)
    if len(outs) == 1:
        outs[0][...] = total
    else:
        first, half = place_ref[1] == 0, outs[0].shape[0]
        outs[0][...] = jnp.where(first, total[:half], total[half:])
        outs[1][...] = jnp.where(first, total[half:], total[:half])


def last_kernel(width, rows, *refs):
    ins, outs, (held, sems) = refs[: len(rows)], refs[len(rows) + 1 : -2], refs[-2:]
    fetch(ins, rows, held, sems)
    for a, out in enumerate(outs):
        total = held[0, :, a * width : (a + 1) * width].astype(F32)
        for i in range(1, len(rows)):
            total = total + held[i, :, a * width : (a + 1) * width].astype(F32)
        out[...] = total


def combine_kernel(in_ref, s_ref, gates_ref, grad_ref, gate_ref, pieces):
    peers = in_ref.shape[0] // ROWS8
    tokens = grad_ref.shape[0]
    width = pieces.shape[1]
    block = s_ref.shape[2]
    moved = mm(by_sublane(peers), in_ref[...]).astype(BF16)
    unpack(moved, pieces, peers, 0)
    picks = s_ref[0] + s_ref[1]
    total = tr_mm(picks, pieces[...]).astype(BF16)
    for j in range(SUB):
        grad_ref[:, j * width : (j + 1) * width] = total[j * tokens : (j + 1) * tokens, :]
    gates = moved[: CAP * peers, CAP * LANE :]
    rows = [tr_mm(gates, s_ref[k])[0:1] for k in range(TOP)]
    rows = jnp.concatenate(rows + [jnp.zeros((8 - TOP, block), F32)], axis=0).astype(BF16)
    rows = mm_tr(rows, natural_order(block))
    gate_ref[...] = (rows[:TOP] / gates_ref[...].astype(F32)).astype(BF16)


def call(kernel, out, ins, scratch, flops, moved, limit=16, place=VMEM):
    return pl.pallas_call(
        kernel,
        out_shape=out,
        in_specs=ins,
        out_specs=jax.tree.map(lambda _: place, out),
        scratch_shapes=scratch,
        compiler_params=pltpu.CompilerParams(vmem_limit_bytes=limit << 20),
        cost_estimate=pl.CostEstimate(flops=flops, bytes_accessed=moved, transcendentals=0),
    )


def shape(*dims, dtype=BF16):
    return jax.ShapeDtypeStruct(dims, dtype)


def dispatch(layer_input, out_grad, ids, gates, peers):
    tokens, depth = layer_input.shape
    block = tokens * SUB
    rows = peers * CAP
    width = depth // SUB
    size = (peers * ROWS8, 2 * CAP * LANE)
    return call(
        dispatch_kernel,
        (shape(*size), shape(TOP, rows, block)),
        [HBM] * 4,
        [
            pltpu.VMEM((tokens, depth), BF16),
            pltpu.VMEM((tokens, depth), BF16),
            pltpu.VMEM((TOP, block), jnp.int32),
            pltpu.VMEM((TOP, block), BF16),
            pltpu.VMEM((block, width), BF16),
            pltpu.VMEM((2, rows, block), BF16),
            pltpu.VMEM(size, BF16),
            pltpu.SemaphoreType.DMA((4,)),
        ],
        flops=10**9,
        moved=4 << 20,
        limit=60,
    )(layer_input, out_grad, ids, gates)


def hidden_part(place, received, w_up, w_down):
    peers = received.shape[0] // ROWS8
    width = w_up.shape[0]
    rows = peers * CAP
    return call(
        hidden_kernel,
        (shape(rows, width),) * 4 + (shape(rows, LANE), shape(width // N_CHIP, 2 * width)),
        [SMEM, VMEM, HBM, HBM],
        [
            pltpu.VMEM(received.shape, BF16),
            pltpu.VMEM(w_up.shape, BF16),
            pltpu.VMEM(w_down.shape, BF16),
            pltpu.SemaphoreType.DMA((3,)),
        ],
        flops=3 * 10**9,
        moved=8 << 20,
        limit=48,
    )(place, received, w_up, w_down)


def blocks(place, arrays, w_up, after):
    rows, width = arrays[0].shape
    peers = rows // CAP
    back = (peers * ROWS8, (CAP + 1) * LANE)
    kept = (width // 2 - width // N_CHIP // 2, 2 * width)
    return call(
        blocks_kernel,
        (shape(*back), shape(*kept), shape(*kept)),
        [SMEM] + [VMEM] * 5 + [HBM, ANY],
        [
            pltpu.VMEM(w_up.shape, BF16),
            pltpu.VMEM(back, BF16),
            pltpu.VMEM(back, BF16),
            pltpu.VMEM((rows, 2 * width // N_CHIP), BF16),
            pltpu.VMEM(kept, BF16),
            pltpu.VMEM(kept, BF16),
            pltpu.SemaphoreType.DMA((4,)),
        ],
        flops=4 * 10**9,
        moved=8 << 20,
        limit=50,
        place=ANY,
    )(place, *arrays, w_up, after)


def ring_step(place, terms, parts):
    arrays, starts = zip(*terms)
    width = arrays[0].shape[1]
    rows = width // 2 // N_CHIP
    return call(
        functools.partial(step_kernel, starts),
        (shape(rows // parts, width),) * parts,
        [SMEM] + [ANY] * len(arrays),
        [pltpu.VMEM((len(arrays), rows, width), BF16), pltpu.SemaphoreType.DMA((len(arrays),))],
        flops=10**6,
        moved=1 << 20,
        limit=52,
    )(place, *arrays)


def finish(half, terms, after):
    arrays, rows = zip(*terms)
    width = arrays[0].shape[1]
    return call(
        functools.partial(last_kernel, width // 2, rows),
        (shape(half, width // 2, dtype=F32),) * 2,
        [ANY] * (len(arrays) + 1),
        [pltpu.VMEM((len(arrays), half, width), BF16), pltpu.SemaphoreType.DMA((len(arrays),))],
        flops=10**6,
        moved=1 << 20,
        limit=52,
    )(*arrays, after)


def combine(returned, picks, gates, tokens, width):
    return call(
        combine_kernel,
        (shape(tokens, SUB * width), shape(TOP, tokens * SUB)),
        [VMEM] * 3,
        [pltpu.VMEM((picks.shape[1], width), BF16)],
        flops=10**10,
        moved=2 << 20,
    )(returned, picks, gates)


def body(n_dp, layer_input, out_grad, expert_ids, gates, up_weight, down_weight):
    tokens = layer_input.shape[0]
    width = up_weight.shape[1]
    peers = lax.axis_size("expert")
    at = lax.axis_index("dp")
    place = jnp.stack([at // 2, at % 2]).astype(jnp.int32)
    gates_t = gates.T
    w_up, w_down = up_weight[0], down_weight[0]

    def exchange(array):
        moved = lax.all_to_all(
            array.reshape(peers, ROWS8, -1), "expert", split_axis=0, concat_axis=0, tiled=True
        )
        return moved.reshape(array.shape)

    def along(array, first_only=False, cross=0):
        pairs = []
        for i in range(n_dp):
            chip, core = i // 2, i % 2
            if core == 0 or not first_only:
                pairs.append((i, (chip + (1 - 2 * core)) % N_CHIP * 2 + (core ^ cross)))
        return lax.ppermute(array, "dp", pairs)

    def swap(array):
        return lax.ppermute(array, "dp", [(i, i ^ 1) for i in range(n_dp)])

    sent, picks = dispatch(layer_input, out_grad, expert_ids.T, gates_t, peers)
    received = exchange(sent)
    *arrays, far = hidden_part(place, received, w_up, w_down)
    got_far = swap(far)
    (total,) = ring_step(place, [(far, 0), (got_far, 0)], 1)
    back, own, other = blocks(place, arrays, w_up, total)
    got = swap(other)
    returned = exchange(back)
    input_grad, gate_grad = combine(returned, picks, gates_t, tokens, width)
    piece = far.shape[0]
    total = along(total, first_only=True)
    last = N_CHIP // 2 - 2
    for r in range(last + 1):
        terms = [(own, r * piece), (got, r * piece), (total, 0)]
        if r < last:
            (total,) = ring_step(place, terms, 1)
            total = along(total)
    same, crossed = ring_step(place, terms, 2)
    same, crossed = along(same), along(crossed, cross=1)
    row = (last + 1) * piece
    up_grad, down_grad = finish(
        piece // 2, [(own, row), (got, row), (same, 0), (crossed, 0)], gate_grad
    )
    return (input_grad, gate_grad.T, up_grad[None], down_grad[None])


def solution(mesh):
    placed = (
        P(("dp", "expert"), None),
        P(("dp", "expert"), None),
        P(("dp", "expert"), None),
        P(("dp", "expert"), None),
        P("expert", None, None),
        P("expert", None, None),
    )
    return jax.shard_map(
        functools.partial(body, mesh.shape["dp"]),
        mesh=mesh,
        in_specs=placed,
        out_specs=(
            P(("dp", "expert"), None),
            P(("dp", "expert"), None),
            P("expert", "dp", None),
            P("expert", "dp", None),
        ),
        check_vma=False,
    )
```

```python
import functools

import jax
import jax.numpy as jnp
from jax import lax
from jax.experimental import pallas as pl
from jax.experimental.pallas import tpu as pltpu
from jax.sharding import PartitionSpec as P

TOP = 2
SUB = 4
CAP = 5
LANE = 128
ROWS8 = 8
N_CHIP = 8
F32 = jnp.float32
BF16 = jnp.bfloat16
VMEM = pl.BlockSpec(memory_space=pltpu.VMEM)
SMEM = pl.BlockSpec(memory_space=pltpu.SMEM)
HBM = pl.BlockSpec(memory_space=pltpu.HBM)
ANY = pl.BlockSpec(memory_space=pl.ANY)


def iota(shape, dim):
    return lax.broadcasted_iota(jnp.int32, shape, dim)


def one_hot(mask):
    return jnp.where(mask, 1.0, 0.0).astype(BF16)


def mm(left, right):
    return jnp.dot(left, right, preferred_element_type=F32)


def mm_tr(left, right):
    return lax.dot_general(left, right, (((1,), (1,)), ((), ())), preferred_element_type=F32)


def tr_mm(left, right):
    return lax.dot_general(left, right, (((0,), (0,)), ((), ())), preferred_element_type=F32)


def by_sublane(peers):
    size = peers * ROWS8
    row, col = iota((size, size), 0), iota((size, size), 1)
    return one_hot(col == lax.rem(row, peers) * ROWS8 + lax.div(row, peers))


def by_peer(peers):
    size = peers * ROWS8
    row, col = iota((size, size), 0), iota((size, size), 1)
    return one_hot(col == lax.rem(row, ROWS8) * peers + lax.div(row, ROWS8))


def natural_order(block):
    tokens = block // SUB
    row, col = iota((block, block), 0), iota((block, block), 1)
    return one_hot(row == lax.rem(col, tokens) * SUB + lax.div(col, tokens))


def dispatch_kernel(
    x_hbm, g_hbm, ids_hbm, gates_hbm, out_ref, s_ref,
    x_ref, g_ref, ids_ref, gates_ref, rows, picks, packed, sems,
):
    tokens = x_ref.shape[0]
    pairs = (
        (ids_hbm, ids_ref), (gates_hbm, gates_ref), (x_hbm, x_ref), (g_hbm, g_ref),
    )
    copies = [pltpu.make_async_copy(a, b, sems.at[i]) for i, (a, b) in enumerate(pairs)]
    for copy in copies:
        copy.start()
    copies[0].wait()
    copies[1].wait()
    block = ids_ref.shape[1]
    peers = out_ref.shape[0] // ROWS8
    width = rows.shape[1]
    chunks = width // LANE
    top = jnp.concatenate(
        [ids_ref[...].astype(F32), gates_ref[...].astype(F32), jnp.zeros((4, block), F32)], axis=0
    ).astype(BF16)
    top = mm(top, natural_order(block))
    expert = iota((peers, block), 0).astype(F32)
    hot = [expert == top[k : k + 1] for k in range(TOP)]
    chosen = one_hot(hot[0] | hot[1])
    earlier = one_hot(iota((block, block), 0) < iota((block, block), 1))
    before = mm(chosen, earlier)
    weight = jnp.where(hot[0], top[2:3], jnp.where(hot[1], top[3:4], 0.0))
    for c in range(CAP):
        slot = pl.ds(c * peers, peers)
        here = before == float(c)
        for k in range(TOP):
            s_ref[k, slot, :] = one_hot(hot[k] & here)
        picks[0, slot, :] = one_hot((hot[0] | hot[1]) & here)
        picks[1, slot, :] = jnp.where(here, weight, 0.0).astype(BF16)
    for a, ref in enumerate((x_ref, g_ref)):
        copies[2 + a].wait()
        for j in range(SUB):
            rows[j * tokens : (j + 1) * tokens, :] = ref[:, j * width : (j + 1) * width]
        sent = mm(picks[a], rows[...]).astype(BF16)
        for c in range(CAP):
            for j in range(chunks):
                packed[j * peers : (j + 1) * peers, (a * CAP + c) * LANE : (a * CAP + c + 1) * LANE] = (
                    sent[c * peers : (c + 1) * peers, j * LANE : (j + 1) * LANE]
                )
    out_ref[...] = mm(by_peer(peers), packed[...]).astype(BF16)


def unpack(source, target, peers, base):
    chunks = target.shape[1] // LANE
    for c in range(CAP):
        for j in range(chunks):
            target[c * peers : (c + 1) * peers, j * LANE : (j + 1) * LANE] = source[
                j * peers : (j + 1) * peers, (base + c) * LANE : (base + c + 1) * LANE
            ]


def hidden_kernel(place_ref, in_hbm, up_hbm, down_hbm, *refs):
    feat, scal, hid, hg_ref, part_ref, far_ref, in_ref, up_ref, down_ref, sems = refs
    pairs = ((in_hbm, in_ref), (up_hbm, up_ref), (down_hbm, down_ref))
    copies = [pltpu.make_async_copy(a, b, sems.at[i]) for i, (a, b) in enumerate(pairs)]
    for copy in copies:
        copy.start()
    peers = in_ref.shape[0] // ROWS8
    width = up_ref.shape[0]
    to_sublane = by_sublane(peers)
    copies[0].wait()
    moved = mm(to_sublane, in_ref[...]).astype(BF16)
    unpack(moved, feat, peers, 0)
    unpack(moved, scal, peers, CAP)
    copies[1].wait()
    pre = mm(feat[...], up_ref[...])
    sig = jax.nn.sigmoid(pre)
    hidden = (pre * sig).astype(BF16)
    hid[...] = hidden
    copies[2].wait()
    back = mm_tr(scal[...], down_ref[...])
    part = jnp.sum(hidden.astype(F32) * back, axis=1, keepdims=True)
    part_ref[...] = jnp.broadcast_to(part, part_ref.shape).astype(BF16)
    hg_ref[...] = (back * (sig * (1.0 + pre * (1.0 - sig)))).astype(BF16)
    here = rows_of(place_ref, N_CHIP // 2, width)
    far_ref[:, :width] = tr_mm(feat[:, here], hg_ref[...]).astype(BF16)
    far_ref[:, width:] = tr_mm(hid[:, here], scal[...]).astype(BF16)


def rows_of(place_ref, offset, width):
    piece = width // N_CHIP
    at = lax.rem(place_ref[0] + offset, N_CHIP) * piece
    return pl.ds(pl.multiple_of(at, piece), piece)


def pieces_kernel(hg_ref, part_ref, up_hbm, _, out_ref, up_ref, packed, sem):
    load = pltpu.make_async_copy(up_hbm, up_ref, sem)
    load.start()
    peers = packed.shape[0] // ROWS8
    rows = CAP * peers
    packed[:rows, CAP * LANE :] = part_ref[...]
    packed[rows:, CAP * LANE :] = jnp.zeros((packed.shape[0] - rows, LANE), BF16)
    to_peer = by_peer(peers)
    load.wait()
    sent = mm_tr(hg_ref[...], up_ref[...]).astype(BF16)
    for c in range(CAP):
        for j in range(up_ref.shape[0] // LANE):
            packed[j * peers : (j + 1) * peers, c * LANE : (c + 1) * LANE] = sent[
                c * peers : (c + 1) * peers, j * LANE : (j + 1) * LANE
            ]
    out_ref[...] = mm(to_peer, packed[...]).astype(BF16)


def presum_kernel(skip, own_hbm, got_hbm, _, out_ref, own, got, sems):
    size = out_ref.shape[0] // 5
    copies = []
    for i in range(5):
        for k, (a, b) in enumerate(((own_hbm, own), (got_hbm, got))):
            source = a.at[pl.ds(skip + i * size, size)]
            copies.append(pltpu.make_async_copy(source, b.at[pl.ds(i * size, size)], sems.at[2 * i + k]))
            copies[-1].start()
    for i in range(5):
        here = slice(i * size, (i + 1) * size)
        copies[2 * i].wait()
        copies[2 * i + 1].wait()
        out_ref[here, :] = (own[here, :].astype(F32) + got[here, :].astype(F32)).astype(BF16)


def blocks_kernel(place_ref, feat, scal, hid, hg_ref, _, *refs):
    own_ref, other_ref, mark_ref, left, own, other, sems = refs
    leaving = []

    def leave(source, target):
        leaving.append(pltpu.make_async_copy(source, target, sems.at[len(leaving)]))
        leaving[-1].start()

    width = feat.shape[1]
    piece = width // N_CHIP
    half = piece // 2
    first = place_ref[1] == 0
    middle = N_CHIP // 2
    for r in range(1, middle):
        near = jnp.where(first, middle - r, middle + r)
        rows = slice((r - 1) * piece, r * piece)
        for a, (source, right) in enumerate(((feat, hg_ref), (hid, scal))):
            left[:, :piece] = source[:, rows_of(place_ref, near, width)]
            left[:, piece:] = source[:, rows_of(place_ref, N_CHIP - near, width)]
            total = tr_mm(left[...], right[...]).astype(BF16)
            lanes = slice(a * width, (a + 1) * width)
            own[rows, lanes] = total[:piece]
            other[rows, lanes] = total[piece:]
    rows = slice((middle - 1) * piece, (middle - 1) * piece + half)
    for a, (source, right) in enumerate(((feat, hg_ref), (hid, scal))):
        total = tr_mm(source[:, rows_of(place_ref, 0, width)], right[...]).astype(BF16)
        lanes = slice(a * width, (a + 1) * width)
        own[rows, lanes] = jnp.where(first, total[:half], total[half:])
        other[rows, lanes] = jnp.where(first, total[half:], total[:half])
    leave(other, other_ref)
    leave(own, own_ref)
    leave(left.at[pl.ds(0, 2 * ROWS8), pl.ds(0, LANE)], mark_ref)
    for copy in leaving:
        copy.wait()


def fetch(refs, rows, held, sems):
    copies = [
        pltpu.make_async_copy(ref.at[pl.ds(row, held.shape[1])], held.at[i], sems.at[i])
        for i, (ref, row) in enumerate(zip(refs, rows))
    ]
    for copy in copies:
        copy.start()
    for copy in copies:
        copy.wait()


def step_kernel(rows, place_ref, *refs):
    ins, outs, (held, sems) = refs[: len(rows)], refs[len(rows) : -2], refs[-2:]
    fetch(ins, rows, held, sems)
    total = held[0].astype(F32)
    for i in range(1, len(rows)):
        total = total + held[i].astype(F32)
    total = total.astype(BF16)
    if len(outs) == 1:
        outs[0][...] = total
    else:
        first, half = place_ref[1] == 0, outs[0].shape[0]
        outs[0][...] = jnp.where(first, total[:half], total[half:])
        outs[1][...] = jnp.where(first, total[half:], total[:half])


def last_kernel(width, rows, *refs):
    ins, outs, (held, sems) = refs[: len(rows)], refs[len(rows) : -2], refs[-2:]
    fetch(ins, rows, held, sems)
    for a, out in enumerate(outs):
        total = held[0, :, a * width : (a + 1) * width].astype(F32)
        for i in range(1, len(rows)):
            total = total + held[i, :, a * width : (a + 1) * width].astype(F32)
        out[...] = total


def combine_kernel(in_ref, s_ref, gates_ref, grad_ref, gate_ref, pieces):
    peers = in_ref.shape[0] // ROWS8
    tokens = grad_ref.shape[0]
    width = pieces.shape[1]
    block = s_ref.shape[2]
    moved = mm(by_sublane(peers), in_ref[...]).astype(BF16)
    unpack(moved, pieces, peers, 0)
    picks = s_ref[0] + s_ref[1]
    total = tr_mm(picks, pieces[...]).astype(BF16)
    for j in range(SUB):
        grad_ref[:, j * width : (j + 1) * width] = total[j * tokens : (j + 1) * tokens, :]
    gates = moved[: CAP * peers, CAP * LANE :]
    rows = [tr_mm(gates, s_ref[k])[0:1] for k in range(TOP)]
    rows = jnp.concatenate(rows + [jnp.zeros((8 - TOP, block), F32)], axis=0).astype(BF16)
    rows = mm_tr(rows, natural_order(block))
    gate_ref[...] = (rows[:TOP] / gates_ref[...].astype(F32)).astype(BF16)


def call(kernel, out, ins, scratch, flops, moved, limit=16, place=VMEM):
    return pl.pallas_call(
        kernel,
        out_shape=out,
        in_specs=ins,
        out_specs=jax.tree.map(lambda _: place, out),
        scratch_shapes=scratch,
        compiler_params=pltpu.CompilerParams(vmem_limit_bytes=limit << 20),
        cost_estimate=pl.CostEstimate(flops=flops, bytes_accessed=moved, transcendentals=0),
    )


def shape(*dims, dtype=BF16):
    return jax.ShapeDtypeStruct(dims, dtype)


def dispatch(layer_input, out_grad, ids, gates, peers):
    tokens, depth = layer_input.shape
    block = tokens * SUB
    rows = peers * CAP
    width = depth // SUB
    size = (peers * ROWS8, 2 * CAP * LANE)
    return call(
        dispatch_kernel,
        (shape(*size), shape(TOP, rows, block)),
        [HBM] * 4,
        [
            pltpu.VMEM((tokens, depth), BF16),
            pltpu.VMEM((tokens, depth), BF16),
            pltpu.VMEM((TOP, block), jnp.int32),
            pltpu.VMEM((TOP, block), BF16),
            pltpu.VMEM((block, width), BF16),
            pltpu.VMEM((2, rows, block), BF16),
            pltpu.VMEM(size, BF16),
            pltpu.SemaphoreType.DMA((4,)),
        ],
        flops=10**9,
        moved=4 << 20,
        limit=60,
    )(layer_input, out_grad, ids, gates)


def hidden_part(place, received, w_up, w_down):
    peers = received.shape[0] // ROWS8
    width = w_up.shape[0]
    rows = peers * CAP
    return call(
        hidden_kernel,
        (shape(rows, width),) * 4 + (shape(rows, LANE), shape(width // N_CHIP, 2 * width)),
        [SMEM, VMEM, HBM, HBM],
        [
            pltpu.VMEM(received.shape, BF16),
            pltpu.VMEM(w_up.shape, BF16),
            pltpu.VMEM(w_down.shape, BF16),
            pltpu.SemaphoreType.DMA((3,)),
        ],
        flops=3 * 10**9,
        moved=8 << 20,
        limit=48,
    )(place, received, w_up, w_down)


def blocks(place, arrays, after):
    rows, width = arrays[0].shape
    kept = (width // 2 - width // N_CHIP // 2, 2 * width)
    return call(
        blocks_kernel,
        (shape(*kept), shape(*kept), shape(2 * ROWS8, LANE)),
        [SMEM] + [VMEM] * 4 + [ANY],
        [
            pltpu.VMEM((rows, 2 * width // N_CHIP), BF16),
            pltpu.VMEM(kept, BF16),
            pltpu.VMEM(kept, BF16),
            pltpu.SemaphoreType.DMA((3,)),
        ],
        flops=3 * 10**9,
        moved=8 << 20,
        limit=50,
        place=ANY,
    )(place, *arrays, after)


def pieces(hidden_grad, part, w_up, after):
    rows, width = hidden_grad.shape
    back = (rows // CAP * ROWS8, (CAP + 1) * LANE)
    return call(
        pieces_kernel,
        shape(*back),
        [VMEM, VMEM, HBM, ANY],
        [pltpu.VMEM(w_up.shape, BF16), pltpu.VMEM(back, BF16), pltpu.SemaphoreType.DMA],
        flops=2 * 10**9,
        moved=4 << 20,
        limit=50,
    )(hidden_grad, part, w_up, after)


def presum(own, got, skip, after):
    size = (own.shape[0] - skip, own.shape[1])
    return call(
        functools.partial(presum_kernel, skip),
        shape(*size),
        [ANY] * 3,
        [pltpu.VMEM(size, BF16)] * 2 + [pltpu.SemaphoreType.DMA((10,))],
        flops=2 * 10**9,
        moved=8 << 20,
        limit=52,
    )(own, got, after)


def ring_step(place, terms, parts):
    arrays, starts = zip(*terms)
    width = arrays[0].shape[1]
    rows = width // 2 // N_CHIP
    return call(
        functools.partial(step_kernel, starts),
        (shape(rows // parts, width),) * parts,
        [SMEM] + [ANY] * len(arrays),
        [pltpu.VMEM((len(arrays), rows, width), BF16), pltpu.SemaphoreType.DMA((len(arrays),))],
        flops=10**6,
        moved=1 << 20,
        limit=52 if len(arrays) > 2 else 49,
    )(place, *arrays)


def finish(half, terms):
    arrays, rows = zip(*terms)
    width = arrays[0].shape[1]
    return call(
        functools.partial(last_kernel, width // 2, rows),
        (shape(half, width // 2, dtype=F32),) * 2,
        [ANY] * len(arrays),
        [pltpu.VMEM((len(arrays), half, width), BF16), pltpu.SemaphoreType.DMA((len(arrays),))],
        flops=10**6,
        moved=1 << 20,
        limit=49,
    )(*arrays)


def combine(returned, picks, gates, tokens, width):
    return call(
        combine_kernel,
        (shape(tokens, SUB * width), shape(TOP, tokens * SUB)),
        [VMEM] * 3,
        [pltpu.VMEM((picks.shape[1], width), BF16)],
        flops=10**10,
        moved=2 << 20,
    )(returned, picks, gates)


def body(n_dp, layer_input, out_grad, expert_ids, gates, up_weight, down_weight):
    tokens = layer_input.shape[0]
    width = up_weight.shape[1]
    peers = lax.axis_size("expert")
    at = lax.axis_index("dp")
    place = jnp.stack([at // 2, at % 2]).astype(jnp.int32)
    gates_t = gates.T
    w_up, w_down = up_weight[0], down_weight[0]

    def exchange(array):
        moved = lax.all_to_all(
            array.reshape(peers, ROWS8, -1), "expert", split_axis=0, concat_axis=0, tiled=True
        )
        return moved.reshape(array.shape)

    def along(array, first_only=False, cross=0):
        pairs = []
        for i in range(n_dp):
            chip, core = i // 2, i % 2
            if core == 0 or not first_only:
                pairs.append((i, (chip + (1 - 2 * core)) % N_CHIP * 2 + (core ^ cross)))
        return lax.ppermute(array, "dp", pairs)

    def swap(array):
        return lax.ppermute(array, "dp", [(i, i ^ 1) for i in range(n_dp)])

    sent, picks = dispatch(layer_input, out_grad, expert_ids.T, gates_t, peers)
    received = exchange(sent)
    *arrays, far = hidden_part(place, received, w_up, w_down)
    got_far = swap(far)
    (total,) = ring_step(place, [(far, 0), (got_far, 0)], 1)
    own, other, mark = blocks(place, arrays[:4], total)
    got = swap(other)
    back = pieces(arrays[3], arrays[4], w_up, mark)
    returned = exchange(back)
    input_grad, gate_grad = combine(returned, picks, gates_t, tokens, width)
    piece = far.shape[0]
    total = along(total, first_only=True)
    (total,) = ring_step(place, [(own, 0), (got, 0), (total, 0)], 1)
    summed = presum(own, got, piece, total)
    total = along(total)
    (total,) = ring_step(place, [(summed, 0), (total, 0)], 1)
    total = along(total)
    same, crossed = ring_step(place, [(summed, piece), (total, 0)], 2)
    same, crossed = along(same), along(crossed, cross=1)
    row = 2 * piece
    up_grad, down_grad = finish(
        piece // 2, [(summed, row), (same, 0), (crossed, 0)]
    )
    return (input_grad, gate_grad.T, up_grad[None], down_grad[None])


def solution(mesh):
    placed = (
        P(("dp", "expert"), None),
        P(("dp", "expert"), None),
        P(("dp", "expert"), None),
        P(("dp", "expert"), None),
        P("expert", None, None),
        P("expert", None, None),
    )
    return jax.shard_map(
        functools.partial(body, mesh.shape["dp"]),
        mesh=mesh,
        in_specs=placed,
        out_specs=(
            P(("dp", "expert"), None),
            P(("dp", "expert"), None),
            P("expert", "dp", None),
            P("expert", "dp", None),
        ),
        check_vma=False,
    )
```

```python
import functools

import jax
import jax.numpy as jnp
from jax import lax
from jax.experimental import pallas as pl
from jax.experimental.pallas import tpu as pltpu
from jax.sharding import PartitionSpec as P

TOP = 2
SUB = 4
CAP = 5
LANE = 128
ROWS8 = 8
N_CHIP = 8
CUTS = 4
F32 = jnp.float32
BF16 = jnp.bfloat16
VMEM = pl.BlockSpec(memory_space=pltpu.VMEM)
SMEM = pl.BlockSpec(memory_space=pltpu.SMEM)
HBM = pl.BlockSpec(memory_space=pltpu.HBM)
ANY = pl.BlockSpec(memory_space=pl.ANY)


def iota(shape, dim):
    return lax.broadcasted_iota(jnp.int32, shape, dim)


def one_hot(mask):
    return jnp.where(mask, 1.0, 0.0).astype(BF16)


def mm(left, right):
    return jnp.dot(left, right, preferred_element_type=F32)


def mm_tr(left, right):
    return lax.dot_general(left, right, (((1,), (1,)), ((), ())), preferred_element_type=F32)


def tr_mm(left, right):
    return lax.dot_general(left, right, (((0,), (0,)), ((), ())), preferred_element_type=F32)


def by_sublane(peers):
    size = peers * ROWS8
    row, col = iota((size, size), 0), iota((size, size), 1)
    return one_hot(col == lax.rem(row, peers) * ROWS8 + lax.div(row, peers))


def by_peer(peers):
    size = peers * ROWS8
    row, col = iota((size, size), 0), iota((size, size), 1)
    return one_hot(col == lax.rem(row, ROWS8) * peers + lax.div(row, ROWS8))


def natural_order(block):
    tokens = block // SUB
    row, col = iota((block, block), 0), iota((block, block), 1)
    return one_hot(row == lax.rem(col, tokens) * SUB + lax.div(col, tokens))


def dispatch_kernel(
    x_hbm, g_hbm, ids_hbm, gates_hbm, out_ref, s_ref,
    x_ref, g_ref, ids_ref, gates_ref, rows, picks, packed, sems,
):
    tokens = x_ref.shape[0]
    pairs = (
        (ids_hbm, ids_ref), (gates_hbm, gates_ref), (x_hbm, x_ref), (g_hbm, g_ref),
    )
    copies = [pltpu.make_async_copy(a, b, sems.at[i]) for i, (a, b) in enumerate(pairs)]
    for copy in copies:
        copy.start()
    in_order = natural_order(ids_ref.shape[1])
    to_peer = by_peer(out_ref.shape[0] // ROWS8)
    copies[0].wait()
    copies[1].wait()
    block = ids_ref.shape[1]
    peers = out_ref.shape[0] // ROWS8
    width = rows.shape[1]
    chunks = width // LANE
    top = jnp.concatenate(
        [ids_ref[...].astype(F32), gates_ref[...].astype(F32), jnp.zeros((4, block), F32)], axis=0
    ).astype(BF16)
    top = mm(top, in_order)
    expert = iota((peers, block), 0).astype(F32)
    hot = [expert == top[k : k + 1] for k in range(TOP)]
    chosen = one_hot(hot[0] | hot[1])
    earlier = one_hot(iota((block, block), 0) < iota((block, block), 1))
    before = mm(chosen, earlier)
    weight = jnp.where(hot[0], top[2:3], jnp.where(hot[1], top[3:4], 0.0))
    for c in range(CAP):
        slot = pl.ds(c * peers, peers)
        here = before == float(c)
        for k in range(TOP):
            s_ref[k, slot, :] = one_hot(hot[k] & here)
        picks[0, slot, :] = one_hot((hot[0] | hot[1]) & here)
        picks[1, slot, :] = jnp.where(here, weight, 0.0).astype(BF16)
    for a, ref in enumerate((x_ref, g_ref)):
        copies[2 + a].wait()
        for j in range(SUB):
            rows[j * tokens : (j + 1) * tokens, :] = ref[:, j * width : (j + 1) * width]
        sent = mm(picks[a], rows[...]).astype(BF16)
        for c in range(CAP):
            for j in range(chunks):
                packed[j * peers : (j + 1) * peers, (a * CAP + c) * LANE : (a * CAP + c + 1) * LANE] = (
                    sent[c * peers : (c + 1) * peers, j * LANE : (j + 1) * LANE]
                )
    out_ref[...] = mm(to_peer, packed[...]).astype(BF16)


def unpack(source, target, peers, base):
    chunks = target.shape[1] // LANE
    for c in range(CAP):
        for j in range(chunks):
            target[c * peers : (c + 1) * peers, j * LANE : (j + 1) * LANE] = source[
                j * peers : (j + 1) * peers, (base + c) * LANE : (base + c + 1) * LANE
            ]


def hidden_kernel(place_ref, in_hbm, up_hbm, down_hbm, *refs):
    feat, scal, hid, hg_ref, part_ref, far_ref, in_ref, up_ref, down_ref, sems = refs
    pairs = ((in_hbm, in_ref), (up_hbm, up_ref), (down_hbm, down_ref))
    copies = [pltpu.make_async_copy(a, b, sems.at[i]) for i, (a, b) in enumerate(pairs)]
    for copy in copies:
        copy.start()
    peers = in_ref.shape[0] // ROWS8
    width = up_ref.shape[0]
    to_sublane = by_sublane(peers)
    copies[0].wait()
    moved = mm(to_sublane, in_ref[...]).astype(BF16)
    unpack(moved, feat, peers, 0)
    unpack(moved, scal, peers, CAP)
    copies[1].wait()
    pre = mm(feat[...], up_ref[...])
    sig = jax.nn.sigmoid(pre)
    hidden = (pre * sig).astype(BF16)
    hid[...] = hidden
    copies[2].wait()
    back = mm_tr(scal[...], down_ref[...])
    part = jnp.sum(hidden.astype(F32) * back, axis=1, keepdims=True)
    part_ref[...] = jnp.broadcast_to(part, part_ref.shape).astype(BF16)
    hg_ref[...] = (back * (sig * (1.0 + pre * (1.0 - sig)))).astype(BF16)
    here = rows_of(place_ref, N_CHIP // 2, width)
    far_ref[:, :width] = tr_mm(feat[:, here], hg_ref[...]).astype(BF16)
    far_ref[:, width:] = tr_mm(hid[:, here], scal[...]).astype(BF16)


def rows_of(place_ref, offset, width):
    piece = width // N_CHIP
    at = lax.rem(place_ref[0] + offset, N_CHIP) * piece
    return pl.ds(pl.multiple_of(at, piece), piece)


def pieces_kernel(hg_ref, part_ref, up_hbm, _, out_ref, up_ref, packed, sem):
    load = pltpu.make_async_copy(up_hbm, up_ref, sem)
    load.start()
    peers = packed.shape[0] // ROWS8
    rows = CAP * peers
    packed[:rows, CAP * LANE :] = part_ref[...]
    packed[rows:, CAP * LANE :] = jnp.zeros((packed.shape[0] - rows, LANE), BF16)
    to_peer = by_peer(peers)
    load.wait()
    sent = mm_tr(hg_ref[...], up_ref[...]).astype(BF16)
    for c in range(CAP):
        for j in range(up_ref.shape[0] // LANE):
            packed[j * peers : (j + 1) * peers, c * LANE : (c + 1) * LANE] = sent[
                c * peers : (c + 1) * peers, j * LANE : (j + 1) * LANE
            ]
    out_ref[...] = mm(to_peer, packed[...]).astype(BF16)


def presum_kernel(skip, own_hbm, got_hbm, _, out_ref, own, got, sems):
    size = out_ref.shape[0] // 5
    copies = []
    for i in range(5):
        for k, (a, b) in enumerate(((own_hbm, own), (got_hbm, got))):
            source = a.at[pl.ds(skip + i * size, size)]
            copies.append(pltpu.make_async_copy(source, b.at[pl.ds(i * size, size)], sems.at[2 * i + k]))
            copies[-1].start()
    for i in range(5):
        here = slice(i * size, (i + 1) * size)
        copies[2 * i].wait()
        copies[2 * i + 1].wait()
        out_ref[here, :] = (own[here, :].astype(F32) + got[here, :].astype(F32)).astype(BF16)


def blocks_kernel(place_ref, feat, scal, hid, hg_ref, _, *refs):
    own_ref, other_ref, mark_ref, left, own, other, sems = refs
    leaving = []

    def leave(source, target):
        leaving.append(pltpu.make_async_copy(source, target, sems.at[len(leaving)]))
        leaving[-1].start()

    width = feat.shape[1]
    piece = width // N_CHIP
    half = piece // 2
    first = place_ref[1] == 0
    middle = N_CHIP // 2
    for r in range(1, middle):
        near = jnp.where(first, middle - r, middle + r)
        rows = slice((r - 1) * piece, r * piece)
        for a, (source, right) in enumerate(((feat, hg_ref), (hid, scal))):
            left[:, :piece] = source[:, rows_of(place_ref, near, width)]
            left[:, piece:] = source[:, rows_of(place_ref, N_CHIP - near, width)]
            total = tr_mm(left[...], right[...]).astype(BF16)
            lanes = slice(a * width, (a + 1) * width)
            own[rows, lanes] = total[:piece]
            other[rows, lanes] = total[piece:]
        at = pl.ds((r - 1) * piece, piece)
        leave(other.at[at], other_ref.at[at])
        leave(own.at[at], own_ref.at[at])
    rows = slice((middle - 1) * piece, (middle - 1) * piece + half)
    for a, (source, right) in enumerate(((feat, hg_ref), (hid, scal))):
        total = tr_mm(source[:, rows_of(place_ref, 0, width)], right[...]).astype(BF16)
        lanes = slice(a * width, (a + 1) * width)
        own[rows, lanes] = jnp.where(first, total[:half], total[half:])
        other[rows, lanes] = jnp.where(first, total[half:], total[:half])
    at = pl.ds((middle - 1) * piece, half)
    leave(other.at[at], other_ref.at[at])
    leave(own.at[at], own_ref.at[at])
    leave(left.at[pl.ds(0, 2 * ROWS8), pl.ds(0, LANE)], mark_ref)
    for copy in leaving:
        copy.wait()


def fetch(refs, rows, held, sems):
    copies = [
        pltpu.make_async_copy(ref.at[pl.ds(row, held.shape[1])], held.at[i], sems.at[i])
        for i, (ref, row) in enumerate(zip(refs, rows))
    ]
    for copy in copies:
        copy.start()
    for copy in copies:
        copy.wait()


def step_kernel(rows, place_ref, *refs):
    ins, outs, (held, sems) = refs[: len(rows)], refs[len(rows) : -2], refs[-2:]
    size = held.shape[1] // CUTS
    copies = []
    for at in range(CUTS):
        for i, (ref, row) in enumerate(zip(ins, rows)):
            source = ref.at[pl.ds(row + at * size, size)]
            target = held.at[i, pl.ds(at * size, size)]
            copies.append(pltpu.make_async_copy(source, target, sems.at[len(copies)]))
            copies[-1].start()
    sums = []
    for at in range(CUTS):
        here = slice(at * size, (at + 1) * size)
        total = None
        for i in range(len(rows)):
            copies[at * len(rows) + i].wait()
            term = held[i, here, :].astype(F32)
            total = term if total is None else total + term
        sums.append(total.astype(BF16))
        if len(outs) == 1:
            outs[0][here, :] = sums[-1]
    if len(outs) == 2:
        first = place_ref[1] == 0
        for at in range(CUTS // 2):
            here = slice(at * size, (at + 1) * size)
            low, high = sums[at], sums[at + CUTS // 2]
            outs[0][here, :] = jnp.where(first, low, high)
            outs[1][here, :] = jnp.where(first, high, low)


def last_kernel(width, rows, *refs):
    ins, outs, (held, sems) = refs[: len(rows)], refs[len(rows) : -2], refs[-2:]
    fetch(ins, rows, held, sems)
    for a, out in enumerate(outs):
        total = held[0, :, a * width : (a + 1) * width].astype(F32)
        for i in range(1, len(rows)):
            total = total + held[i, :, a * width : (a + 1) * width].astype(F32)
        out[...] = total


def combine_kernel(in_ref, s_ref, gates_ref, grad_ref, gate_ref, pieces):
    peers = in_ref.shape[0] // ROWS8
    tokens = grad_ref.shape[0]
    width = pieces.shape[1]
    block = s_ref.shape[2]
    moved = mm(by_sublane(peers), in_ref[...]).astype(BF16)
    unpack(moved, pieces, peers, 0)
    picks = s_ref[0] + s_ref[1]
    total = tr_mm(picks, pieces[...]).astype(BF16)
    for j in range(SUB):
        grad_ref[:, j * width : (j + 1) * width] = total[j * tokens : (j + 1) * tokens, :]
    gates = moved[: CAP * peers, CAP * LANE :]
    rows = [tr_mm(gates, s_ref[k])[0:1] for k in range(TOP)]
    rows = jnp.concatenate(rows + [jnp.zeros((8 - TOP, block), F32)], axis=0).astype(BF16)
    rows = mm_tr(rows, natural_order(block))
    gate_ref[...] = (rows[:TOP] / gates_ref[...].astype(F32)).astype(BF16)


def call(kernel, out, ins, scratch, flops, moved, limit=16, place=VMEM):
    return pl.pallas_call(
        kernel,
        out_shape=out,
        in_specs=ins,
        out_specs=jax.tree.map(lambda _: place, out),
        scratch_shapes=scratch,
        compiler_params=pltpu.CompilerParams(vmem_limit_bytes=limit << 20),
        cost_estimate=pl.CostEstimate(flops=flops, bytes_accessed=moved, transcendentals=0),
    )


def shape(*dims, dtype=BF16):
    return jax.ShapeDtypeStruct(dims, dtype)


def dispatch(layer_input, out_grad, ids, gates, peers):
    tokens, depth = layer_input.shape
    block = tokens * SUB
    rows = peers * CAP
    width = depth // SUB
    size = (peers * ROWS8, 2 * CAP * LANE)
    return call(
        dispatch_kernel,
        (shape(*size), shape(TOP, rows, block)),
        [HBM] * 4,
        [
            pltpu.VMEM((tokens, depth), BF16),
            pltpu.VMEM((tokens, depth), BF16),
            pltpu.VMEM((TOP, block), jnp.int32),
            pltpu.VMEM((TOP, block), BF16),
            pltpu.VMEM((block, width), BF16),
            pltpu.VMEM((2, rows, block), BF16),
            pltpu.VMEM(size, BF16),
            pltpu.SemaphoreType.DMA((4,)),
        ],
        flops=10**9,
        moved=4 << 20,
        limit=60,
    )(layer_input, out_grad, ids, gates)


def hidden_part(place, received, w_up, w_down):
    peers = received.shape[0] // ROWS8
    width = w_up.shape[0]
    rows = peers * CAP
    return call(
        hidden_kernel,
        (shape(rows, width),) * 4 + (shape(rows, LANE), shape(width // N_CHIP, 2 * width)),
        [SMEM, VMEM, HBM, HBM],
        [
            pltpu.VMEM(received.shape, BF16),
            pltpu.VMEM(w_up.shape, BF16),
            pltpu.VMEM(w_down.shape, BF16),
            pltpu.SemaphoreType.DMA((3,)),
        ],
        flops=3 * 10**9,
        moved=8 << 20,
        limit=48,
    )(place, received, w_up, w_down)


def blocks(place, arrays, after):
    rows, width = arrays[0].shape
    kept = (width // 2 - width // N_CHIP // 2, 2 * width)
    return call(
        blocks_kernel,
        (shape(*kept), shape(*kept), shape(2 * ROWS8, LANE)),
        [SMEM] + [VMEM] * 4 + [ANY],
        [
            pltpu.VMEM((rows, 2 * width // N_CHIP), BF16),
            pltpu.VMEM(kept, BF16),
            pltpu.VMEM(kept, BF16),
            pltpu.SemaphoreType.DMA((9,)),
        ],
        flops=3 * 10**9,
        moved=8 << 20,
        limit=50,
        place=ANY,
    )(place, *arrays, after)


def pieces(hidden_grad, part, w_up, after):
    rows, width = hidden_grad.shape
    back = (rows // CAP * ROWS8, (CAP + 1) * LANE)
    return call(
        pieces_kernel,
        shape(*back),
        [VMEM, VMEM, HBM, ANY],
        [pltpu.VMEM(w_up.shape, BF16), pltpu.VMEM(back, BF16), pltpu.SemaphoreType.DMA],
        flops=2 * 10**9,
        moved=4 << 20,
        limit=50,
    )(hidden_grad, part, w_up, after)


def presum(own, got, skip, after):
    size = (own.shape[0] - skip, own.shape[1])
    return call(
        functools.partial(presum_kernel, skip),
        shape(*size),
        [ANY] * 3,
        [pltpu.VMEM(size, BF16)] * 2 + [pltpu.SemaphoreType.DMA((10,))],
        flops=2 * 10**9,
        moved=8 << 20,
        limit=52,
    )(own, got, after)


def ring_step(place, terms, parts):
    arrays, starts = zip(*terms)
    width = arrays[0].shape[1]
    rows = width // 2 // N_CHIP
    return call(
        functools.partial(step_kernel, starts),
        (shape(rows // parts, width),) * parts,
        [SMEM] + [ANY] * len(arrays),
        [pltpu.VMEM((len(arrays), rows, width), BF16), pltpu.SemaphoreType.DMA((CUTS * len(arrays),))],
        flops=10**6,
        moved=1 << 20,
        limit=52 if len(arrays) > 2 else 49,
    )(place, *arrays)


def finish(half, terms):
    arrays, rows = zip(*terms)
    width = arrays[0].shape[1]
    return call(
        functools.partial(last_kernel, width // 2, rows),
        (shape(half, width // 2, dtype=F32),) * 2,
        [ANY] * len(arrays),
        [pltpu.VMEM((len(arrays), half, width), BF16), pltpu.SemaphoreType.DMA((len(arrays),))],
        flops=10**6,
        moved=1 << 20,
        limit=49,
    )(*arrays)


def combine(returned, picks, gates, tokens, width):
    return call(
        combine_kernel,
        (shape(tokens, SUB * width), shape(TOP, tokens * SUB)),
        [VMEM] * 3,
        [pltpu.VMEM((picks.shape[1], width), BF16)],
        flops=10**10,
        moved=2 << 20,
    )(returned, picks, gates)


def body(n_dp, layer_input, out_grad, expert_ids, gates, up_weight, down_weight):
    tokens = layer_input.shape[0]
    width = up_weight.shape[1]
    peers = lax.axis_size("expert")
    at = lax.axis_index("dp")
    place = jnp.stack([at // 2, at % 2]).astype(jnp.int32)
    gates_t = gates.T
    w_up, w_down = up_weight[0], down_weight[0]

    def exchange(array):
        moved = lax.all_to_all(
            array.reshape(peers, ROWS8, -1), "expert", split_axis=0, concat_axis=0, tiled=True
        )
        return moved.reshape(array.shape)

    def along(array, first_only=False, cross=0):
        pairs = []
        for i in range(n_dp):
            chip, core = i // 2, i % 2
            if core == 0 or not first_only:
                pairs.append((i, (chip + (1 - 2 * core)) % N_CHIP * 2 + (core ^ cross)))
        return lax.ppermute(array, "dp", pairs)

    def swap(array):
        return lax.ppermute(array, "dp", [(i, i ^ 1) for i in range(n_dp)])

    sent, picks = dispatch(layer_input, out_grad, expert_ids.T, gates_t, peers)
    received = exchange(sent)
    *arrays, far = hidden_part(place, received, w_up, w_down)
    got_far = swap(far)
    (total,) = ring_step(place, [(far, 0), (got_far, 0)], 1)
    own, other, mark = blocks(place, arrays[:4], total)
    got = swap(other)
    back = pieces(arrays[3], arrays[4], w_up, mark)
    returned = exchange(back)
    input_grad, gate_grad = combine(returned, picks, gates_t, tokens, width)
    piece = far.shape[0]
    total = along(total, first_only=True)
    (total,) = ring_step(place, [(own, 0), (got, 0), (total, 0)], 1)
    summed = presum(own, got, piece, total)
    total = along(total)
    (total,) = ring_step(place, [(summed, 0), (total, 0)], 1)
    total = along(total)
    same, crossed = ring_step(place, [(summed, piece), (total, 0)], 2)
    same, crossed = along(same), along(crossed, cross=1)
    row = 2 * piece
    up_grad, down_grad = finish(
        piece // 2, [(summed, row), (same, 0), (crossed, 0)]
    )
    return (input_grad, gate_grad.T, up_grad[None], down_grad[None])


def solution(mesh):
    placed = (
        P(("dp", "expert"), None),
        P(("dp", "expert"), None),
        P(("dp", "expert"), None),
        P(("dp", "expert"), None),
        P("expert", None, None),
        P("expert", None, None),
    )
    return jax.shard_map(
        functools.partial(body, mesh.shape["dp"]),
        mesh=mesh,
        in_specs=placed,
        out_specs=(
            P(("dp", "expert"), None),
            P(("dp", "expert"), None),
            P("expert", "dp", None),
            P("expert", "dp", None),
        ),
        check_vma=False,
    )
```

```python
import functools

import jax
import jax.numpy as jnp
from jax import lax
from jax.experimental import pallas as pl
from jax.experimental.pallas import tpu as pltpu
from jax.sharding import PartitionSpec as P

TOP = 2
SUB = 4
CAP = 5
LANE = 128
ROWS8 = 8
N_CHIP = 8
F32 = jnp.float32
BF16 = jnp.bfloat16
VMEM = pl.BlockSpec(memory_space=pltpu.VMEM)
SMEM = pl.BlockSpec(memory_space=pltpu.SMEM)
HBM = pl.BlockSpec(memory_space=pltpu.HBM)
ANY = pl.BlockSpec(memory_space=pl.ANY)


def iota(shape, dim):
    return lax.broadcasted_iota(jnp.int32, shape, dim)


def one_hot(mask):
    return jnp.where(mask, 1.0, 0.0).astype(BF16)


def mm(left, right):
    return jnp.dot(left, right, preferred_element_type=F32)


def mm_tr(left, right):
    return lax.dot_general(left, right, (((1,), (1,)), ((), ())), preferred_element_type=F32)


def tr_mm(left, right):
    return lax.dot_general(left, right, (((0,), (0,)), ((), ())), preferred_element_type=F32)


def by_sublane(peers):
    size = peers * ROWS8
    row, col = iota((size, size), 0), iota((size, size), 1)
    return one_hot(col == lax.rem(row, peers) * ROWS8 + lax.div(row, peers))


def by_peer(peers):
    size = peers * ROWS8
    row, col = iota((size, size), 0), iota((size, size), 1)
    return one_hot(col == lax.rem(row, ROWS8) * peers + lax.div(row, ROWS8))


def natural_order(block):
    tokens = block // SUB
    row, col = iota((block, block), 0), iota((block, block), 1)
    return one_hot(row == lax.rem(col, tokens) * SUB + lax.div(col, tokens))


def dispatch_kernel(
    x_hbm, g_hbm, ids_hbm, gates_hbm, out_ref, s_ref,
    x_ref, g_ref, ids_ref, gates_ref, rows, picks, packed, sems,
):
    tokens = x_ref.shape[0]
    pairs = (
        (ids_hbm, ids_ref), (gates_hbm, gates_ref), (x_hbm, x_ref), (g_hbm, g_ref),
    )
    copies = [pltpu.make_async_copy(a, b, sems.at[i]) for i, (a, b) in enumerate(pairs)]
    for copy in copies:
        copy.start()
    in_order = natural_order(ids_ref.shape[1])
    to_peer = by_peer(out_ref.shape[0] // ROWS8)
    copies[0].wait()
    copies[1].wait()
    block = ids_ref.shape[1]
    peers = out_ref.shape[0] // ROWS8
    width = rows.shape[1]
    chunks = width // LANE
    top = jnp.concatenate(
        [ids_ref[...].astype(F32), gates_ref[...].astype(F32), jnp.zeros((4, block), F32)], axis=0
    ).astype(BF16)
    top = mm(top, in_order)
    expert = iota((peers, block), 0).astype(F32)
    hot = [expert == top[k : k + 1] for k in range(TOP)]
    chosen = one_hot(hot[0] | hot[1])
    earlier = one_hot(iota((block, block), 0) < iota((block, block), 1))
    before = mm(chosen, earlier)
    weight = jnp.where(hot[0], top[2:3], jnp.where(hot[1], top[3:4], 0.0))
    for c in range(CAP):
        slot = pl.ds(c * peers, peers)
        here = before == float(c)
        for k in range(TOP):
            s_ref[k, slot, :] = one_hot(hot[k] & here)
        picks[0, slot, :] = one_hot((hot[0] | hot[1]) & here)
        picks[1, slot, :] = jnp.where(here, weight, 0.0).astype(BF16)
    for a, ref in enumerate((x_ref, g_ref)):
        copies[2 + a].wait()
        for j in range(SUB):
            rows[j * tokens : (j + 1) * tokens, :] = ref[:, j * width : (j + 1) * width]
        sent = mm(picks[a], rows[...]).astype(BF16)
        for c in range(CAP):
            for j in range(chunks):
                packed[j * peers : (j + 1) * peers, (a * CAP + c) * LANE : (a * CAP + c + 1) * LANE] = (
                    sent[c * peers : (c + 1) * peers, j * LANE : (j + 1) * LANE]
                )
    out_ref[...] = mm(to_peer, packed[...]).astype(BF16)


def unpack(source, target, peers, base):
    chunks = target.shape[1] // LANE
    for c in range(CAP):
        for j in range(chunks):
            target[c * peers : (c + 1) * peers, j * LANE : (j + 1) * LANE] = source[
                j * peers : (j + 1) * peers, (base + c) * LANE : (base + c + 1) * LANE
            ]


def hidden_kernel(place_ref, in_hbm, up_hbm, down_hbm, *refs):
    feat, scal, hid, hg_ref, part_ref, far_ref, in_ref, up_ref, down_ref, sems = refs
    pairs = ((in_hbm, in_ref), (up_hbm, up_ref), (down_hbm, down_ref))
    copies = [pltpu.make_async_copy(a, b, sems.at[i]) for i, (a, b) in enumerate(pairs)]
    for copy in copies:
        copy.start()
    peers = in_ref.shape[0] // ROWS8
    width = up_ref.shape[0]
    to_sublane = by_sublane(peers)
    copies[0].wait()
    moved = mm(to_sublane, in_ref[...]).astype(BF16)
    unpack(moved, feat, peers, 0)
    unpack(moved, scal, peers, CAP)
    copies[1].wait()
    pre = mm(feat[...], up_ref[...])
    sig = jax.nn.sigmoid(pre)
    hidden = (pre * sig).astype(BF16)
    hid[...] = hidden
    copies[2].wait()
    back = mm_tr(scal[...], down_ref[...])
    part = jnp.sum(hidden.astype(F32) * back, axis=1, keepdims=True)
    part_ref[...] = jnp.broadcast_to(part, part_ref.shape).astype(BF16)
    hg_ref[...] = (back * (sig * (1.0 + pre * (1.0 - sig)))).astype(BF16)
    here = rows_of(place_ref, N_CHIP // 2, width)
    far_ref[:, :width] = tr_mm(feat[:, here], hg_ref[...]).astype(BF16)
    far_ref[:, width:] = tr_mm(hid[:, here], scal[...]).astype(BF16)


def rows_of(place_ref, offset, width):
    piece = width // N_CHIP
    at = lax.rem(place_ref[0] + offset, N_CHIP) * piece
    return pl.ds(pl.multiple_of(at, piece), piece)


def pieces_kernel(hg_ref, part_ref, up_hbm, _, out_ref, up_ref, packed, sem):
    load = pltpu.make_async_copy(up_hbm, up_ref, sem)
    load.start()
    peers = packed.shape[0] // ROWS8
    rows = CAP * peers
    packed[:rows, CAP * LANE :] = part_ref[...]
    packed[rows:, CAP * LANE :] = jnp.zeros((packed.shape[0] - rows, LANE), BF16)
    to_peer = by_peer(peers)
    load.wait()
    sent = mm_tr(hg_ref[...], up_ref[...]).astype(BF16)
    for c in range(CAP):
        for j in range(up_ref.shape[0] // LANE):
            packed[j * peers : (j + 1) * peers, c * LANE : (c + 1) * LANE] = sent[
                c * peers : (c + 1) * peers, j * LANE : (j + 1) * LANE
            ]
    out_ref[...] = mm(to_peer, packed[...]).astype(BF16)


def presum_kernel(skip, own_hbm, got_hbm, _, out_ref, own, got, sems):
    size = out_ref.shape[0] // 5
    copies = []
    for i in range(5):
        for k, (a, b) in enumerate(((own_hbm, own), (got_hbm, got))):
            source = a.at[pl.ds(skip + i * size, size)]
            copies.append(pltpu.make_async_copy(source, b.at[pl.ds(i * size, size)], sems.at[2 * i + k]))
            copies[-1].start()
    for i in range(5):
        here = slice(i * size, (i + 1) * size)
        copies[2 * i].wait()
        copies[2 * i + 1].wait()
        out_ref[here, :] = (own[here, :].astype(F32) + got[here, :].astype(F32)).astype(BF16)


def blocks_kernel(place_ref, feat, scal, hid, hg_ref, _, *refs):
    own_ref, other_ref, mark_ref, left, own, other, sems = refs
    leaving = []

    def leave(source, target):
        leaving.append(pltpu.make_async_copy(source, target, sems.at[len(leaving)]))
        leaving[-1].start()

    width = feat.shape[1]
    piece = width // N_CHIP
    half = piece // 2
    first = place_ref[1] == 0
    middle = N_CHIP // 2
    for r in range(1, middle):
        near = jnp.where(first, middle - r, middle + r)
        rows = slice((r - 1) * piece, r * piece)
        for a, (source, right) in enumerate(((feat, hg_ref), (hid, scal))):
            left[:, :piece] = source[:, rows_of(place_ref, near, width)]
            left[:, piece:] = source[:, rows_of(place_ref, N_CHIP - near, width)]
            total = tr_mm(left[...], right[...]).astype(BF16)
            lanes = slice(a * width, (a + 1) * width)
            own[rows, lanes] = total[:piece]
            other[rows, lanes] = total[piece:]
        at = pl.ds((r - 1) * piece, piece)
        leave(other.at[at], other_ref.at[at])
        leave(own.at[at], own_ref.at[at])
    rows = slice((middle - 1) * piece, (middle - 1) * piece + half)
    for a, (source, right) in enumerate(((feat, hg_ref), (hid, scal))):
        total = tr_mm(source[:, rows_of(place_ref, 0, width)], right[...]).astype(BF16)
        lanes = slice(a * width, (a + 1) * width)
        own[rows, lanes] = jnp.where(first, total[:half], total[half:])
        other[rows, lanes] = jnp.where(first, total[half:], total[:half])
    at = pl.ds((middle - 1) * piece, half)
    leave(other.at[at], other_ref.at[at])
    leave(own.at[at], own_ref.at[at])
    leave(left.at[pl.ds(0, 2 * ROWS8), pl.ds(0, LANE)], mark_ref)
    for copy in leaving:
        copy.wait()


def fetch(refs, rows, held, sems):
    copies = [
        pltpu.make_async_copy(ref.at[pl.ds(row, held.shape[1])], held.at[i], sems.at[i])
        for i, (ref, row) in enumerate(zip(refs, rows))
    ]
    for copy in copies:
        copy.start()
    for copy in copies:
        copy.wait()


def step_kernel(rows, place_ref, *refs):
    ins, rest = refs[: len(rows)], refs[len(rows) :]
    if len(rows) > 2:
        *outs, held, sems = rest
        fetch(ins, rows, held, sems)
        terms = [held[i].astype(F32) for i in range(len(rows))]
    else:
        outs = rest
        size = outs[0].shape[0] * len(outs)
        terms = [ref[row : row + size, :].astype(F32) for ref, row in zip(ins, rows)]
    total = functools.reduce(jnp.add, terms).astype(BF16)
    if len(outs) == 1:
        outs[0][...] = total
    else:
        first, half = place_ref[1] == 0, outs[0].shape[0]
        outs[0][...] = jnp.where(first, total[:half], total[half:])
        outs[1][...] = jnp.where(first, total[half:], total[:half])


def last_kernel(width, rows, *refs):
    ins, outs, (held, sems) = refs[: len(rows)], refs[len(rows) : -2], refs[-2:]
    fetch(ins, rows, held, sems)
    for a, out in enumerate(outs):
        total = held[0, :, a * width : (a + 1) * width].astype(F32)
        for i in range(1, len(rows)):
            total = total + held[i, :, a * width : (a + 1) * width].astype(F32)
        out[...] = total


def combine_kernel(in_ref, s_ref, gates_ref, grad_ref, gate_ref, pieces):
    peers = in_ref.shape[0] // ROWS8
    tokens = grad_ref.shape[0]
    width = pieces.shape[1]
    block = s_ref.shape[2]
    moved = mm(by_sublane(peers), in_ref[...]).astype(BF16)
    unpack(moved, pieces, peers, 0)
    picks = s_ref[0] + s_ref[1]
    total = tr_mm(picks, pieces[...]).astype(BF16)
    for j in range(SUB):
        grad_ref[:, j * width : (j + 1) * width] = total[j * tokens : (j + 1) * tokens, :]
    gates = moved[: CAP * peers, CAP * LANE :]
    rows = [tr_mm(gates, s_ref[k])[0:1] for k in range(TOP)]
    rows = jnp.concatenate(rows + [jnp.zeros((8 - TOP, block), F32)], axis=0).astype(BF16)
    rows = mm_tr(rows, natural_order(block))
    gate_ref[...] = (rows[:TOP] / gates_ref[...].astype(F32)).astype(BF16)


def call(kernel, out, ins, scratch, flops, moved, limit=16, place=VMEM):
    return pl.pallas_call(
        kernel,
        out_shape=out,
        in_specs=ins,
        out_specs=jax.tree.map(lambda _: place, out),
        scratch_shapes=scratch,
        compiler_params=pltpu.CompilerParams(vmem_limit_bytes=limit << 20),
        cost_estimate=pl.CostEstimate(flops=flops, bytes_accessed=moved, transcendentals=0),
    )


def shape(*dims, dtype=BF16):
    return jax.ShapeDtypeStruct(dims, dtype)


def dispatch(layer_input, out_grad, ids, gates, peers):
    tokens, depth = layer_input.shape
    block = tokens * SUB
    rows = peers * CAP
    width = depth // SUB
    size = (peers * ROWS8, 2 * CAP * LANE)
    return call(
        dispatch_kernel,
        (shape(*size), shape(TOP, rows, block)),
        [HBM] * 4,
        [
            pltpu.VMEM((tokens, depth), BF16),
            pltpu.VMEM((tokens, depth), BF16),
            pltpu.VMEM((TOP, block), jnp.int32),
            pltpu.VMEM((TOP, block), BF16),
            pltpu.VMEM((block, width), BF16),
            pltpu.VMEM((2, rows, block), BF16),
            pltpu.VMEM(size, BF16),
            pltpu.SemaphoreType.DMA((4,)),
        ],
        flops=10**9,
        moved=4 << 20,
        limit=60,
    )(layer_input, out_grad, ids, gates)


def hidden_part(place, received, w_up, w_down):
    peers = received.shape[0] // ROWS8
    width = w_up.shape[0]
    rows = peers * CAP
    return call(
        hidden_kernel,
        (shape(rows, width),) * 4 + (shape(rows, LANE), shape(width // N_CHIP, 2 * width)),
        [SMEM, VMEM, HBM, HBM],
        [
            pltpu.VMEM(received.shape, BF16),
            pltpu.VMEM(w_up.shape, BF16),
            pltpu.VMEM(w_down.shape, BF16),
            pltpu.SemaphoreType.DMA((3,)),
        ],
        flops=3 * 10**9,
        moved=8 << 20,
        limit=48,
    )(place, received, w_up, w_down)


def blocks(place, arrays, after):
    rows, width = arrays[0].shape
    kept = (width // 2 - width // N_CHIP // 2, 2 * width)
    return call(
        blocks_kernel,
        (shape(*kept), shape(*kept), shape(2 * ROWS8, LANE)),
        [SMEM] + [VMEM] * 4 + [ANY],
        [
            pltpu.VMEM((rows, 2 * width // N_CHIP), BF16),
            pltpu.VMEM(kept, BF16),
            pltpu.VMEM(kept, BF16),
            pltpu.SemaphoreType.DMA((9,)),
        ],
        flops=3 * 10**9,
        moved=8 << 20,
        limit=50,
        place=ANY,
    )(place, *arrays, after)


def pieces(hidden_grad, part, w_up, after):
    rows, width = hidden_grad.shape
    back = (rows // CAP * ROWS8, (CAP + 1) * LANE)
    return call(
        pieces_kernel,
        shape(*back),
        [VMEM, VMEM, HBM, ANY],
        [pltpu.VMEM(w_up.shape, BF16), pltpu.VMEM(back, BF16), pltpu.SemaphoreType.DMA],
        flops=2 * 10**9,
        moved=4 << 20,
        limit=50,
    )(hidden_grad, part, w_up, after)


def presum(own, got, skip, after):
    size = (own.shape[0] - skip, own.shape[1])
    return call(
        functools.partial(presum_kernel, skip),
        shape(*size),
        [ANY] * 3,
        [pltpu.VMEM(size, BF16)] * 2 + [pltpu.SemaphoreType.DMA((10,))],
        flops=2 * 10**9,
        moved=8 << 20,
        limit=52,
    )(own, got, after)


def ring_step(place, terms, parts):
    arrays, starts = zip(*terms)
    width = arrays[0].shape[1]
    rows = width // 2 // N_CHIP
    near = len(arrays) <= 2
    held = [pltpu.VMEM((len(arrays), rows, width), BF16), pltpu.SemaphoreType.DMA((len(arrays),))]
    return call(
        functools.partial(step_kernel, starts),
        (shape(rows // parts, width),) * parts,
        [SMEM] + [VMEM if near else ANY] * len(arrays),
        [] if near else held,
        flops=10**6,
        moved=1 << 20,
        limit=49 if near else 52,
    )(place, *arrays)


def finish(half, terms):
    arrays, rows = zip(*terms)
    width = arrays[0].shape[1]
    return call(
        functools.partial(last_kernel, width // 2, rows),
        (shape(half, width // 2, dtype=F32),) * 2,
        [ANY] * len(arrays),
        [pltpu.VMEM((len(arrays), half, width), BF16), pltpu.SemaphoreType.DMA((len(arrays),))],
        flops=10**6,
        moved=1 << 20,
        limit=49,
    )(*arrays)


def combine(returned, picks, gates, tokens, width):
    return call(
        combine_kernel,
        (shape(tokens, SUB * width), shape(TOP, tokens * SUB)),
        [VMEM] * 3,
        [pltpu.VMEM((picks.shape[1], width), BF16)],
        flops=10**10,
        moved=2 << 20,
    )(returned, picks, gates)


def body(n_dp, layer_input, out_grad, expert_ids, gates, up_weight, down_weight):
    tokens = layer_input.shape[0]
    width = up_weight.shape[1]
    peers = lax.axis_size("expert")
    at = lax.axis_index("dp")
    place = jnp.stack([at // 2, at % 2]).astype(jnp.int32)
    gates_t = gates.T
    w_up, w_down = up_weight[0], down_weight[0]

    def exchange(array):
        moved = lax.all_to_all(
            array.reshape(peers, ROWS8, -1), "expert", split_axis=0, concat_axis=0, tiled=True
        )
        return moved.reshape(array.shape)

    def along(array, first_only=False, cross=0):
        pairs = []
        for i in range(n_dp):
            chip, core = i // 2, i % 2
            if core == 0 or not first_only:
                pairs.append((i, (chip + (1 - 2 * core)) % N_CHIP * 2 + (core ^ cross)))
        return lax.ppermute(array, "dp", pairs)

    def swap(array):
        return lax.ppermute(array, "dp", [(i, i ^ 1) for i in range(n_dp)])

    sent, picks = dispatch(layer_input, out_grad, expert_ids.T, gates_t, peers)
    received = exchange(sent)
    *arrays, far = hidden_part(place, received, w_up, w_down)
    got_far = swap(far)
    (total,) = ring_step(place, [(far, 0), (got_far, 0)], 1)
    own, other, mark = blocks(place, arrays[:4], total)
    got = swap(other)
    back = pieces(arrays[3], arrays[4], w_up, mark)
    returned = exchange(back)
    input_grad, gate_grad = combine(returned, picks, gates_t, tokens, width)
    piece = far.shape[0]
    total = along(total, first_only=True)
    (total,) = ring_step(place, [(own, 0), (got, 0), (total, 0)], 1)
    summed = presum(own, got, piece, total)
    total = along(total)
    (total,) = ring_step(place, [(summed, 0), (total, 0)], 1)
    total = along(total)
    same, crossed = ring_step(place, [(summed, piece), (total, 0)], 2)
    same, crossed = along(same), along(crossed, cross=1)
    row = 2 * piece
    up_grad, down_grad = finish(
        piece // 2, [(summed, row), (same, 0), (crossed, 0)]
    )
    return (input_grad, gate_grad.T, up_grad[None], down_grad[None])


def solution(mesh):
    placed = (
        P(("dp", "expert"), None),
        P(("dp", "expert"), None),
        P(("dp", "expert"), None),
        P(("dp", "expert"), None),
        P("expert", None, None),
        P("expert", None, None),
    )
    return jax.shard_map(
        functools.partial(body, mesh.shape["dp"]),
        mesh=mesh,
        in_specs=placed,
        out_specs=(
            P(("dp", "expert"), None),
            P(("dp", "expert"), None),
            P("expert", "dp", None),
            P("expert", "dp", None),
        ),
        check_vma=False,
    )
```
